32 devices in a mesh: tm: 8 (over y, x, core), space: 4 (over z).
Axes of the slice: x: 2, y: 2, z: 4, core: 2. Of those that a mesh axis runs over, the one named last changes fastest.
Arguments:
- clip: bfloat16 [128, 128, 768], P('tm', 'space'), may hold values from -160 to 160
- w_spatial: bfloat16 [4, 768, 768], replicated, may hold values from -4 to 4
- w_temporal: bfloat16 [4, 768, 768], replicated, may hold values from -4 to 4
Outputs:
- result: bfloat16 [128, 128, 768], P('tm', 'space')
The draws below stay inside these ranges and needn't reach their ends.
All inputs are finite; a program needn't handle non-finite values.
Results may differ from the reference program's by a relative error of at most 0.011.
Values may be sent and summed in bfloat16 or wider, within the bound.
No kernel may reach another device: no remote copies, remote signals or barrier semaphores. Data moves between devices by JAX's collectives and lax.ppermute only.
A program may use at most 128 MiB of HBM per device.

```python
import math
import jax
import jax.numpy as jnp
from jax import lax

D = 768
HEAD = 64
HEADS = 12
FRAMES = 128
TOKS = 128


def scaled_normal(key, shape, limit):
    return jnp.clip(jax.random.normal(key, shape, jnp.float32), -limit, limit)


def draw_clip(key, part):
    keys = jax.random.split(jax.random.fold_in(key, 11), 3)
    column = jnp.exp(jax.random.uniform(keys[0], (D,), jnp.float32, 0.0, math.log(10.0)))
    column = column / jnp.sqrt(jnp.mean(column * column))
    row_scale = jnp.exp(jax.random.uniform(keys[1], (FRAMES, TOKS, 1), jnp.float32, math.log(0.3), math.log(3.0)))
    values = scaled_normal(keys[2], (FRAMES, TOKS, D), 5.0)
    return (values * column[None, None, :] * row_scale).astype(jnp.bfloat16)


def attention_weights(key, salt):
    keys = jax.random.split(jax.random.fold_in(key, salt), 1)
    drawn = scaled_normal(keys[0], (4, D, D), 4.0) / math.sqrt(D)
    return drawn.astype(jnp.bfloat16)


def draw_w_spatial(key, part):
    return attention_weights(key, 23)


def draw_w_temporal(key, part):
    return attention_weights(key, 37)


def setup_inputs(seed: int = 0) -> dict:
    streams_of = jax.random.split(jax.random.key(seed), 4)
    clip = draw_clip(jax.random.fold_in(streams_of[3], 71), 0)
    w_spatial = draw_w_spatial(jax.random.fold_in(streams_of[3], 71), 0)
    w_temporal = draw_w_temporal(jax.random.fold_in(streams_of[3], 71), 0)
    return dict(clip=clip, w_spatial=w_spatial, w_temporal=w_temporal)


def rms_norm(values):
    wide = values.astype(jnp.float32)
    return (wide * lax.rsqrt(lax.optimization_barrier(jnp.mean(wide * wide, axis=-1, keepdims=True)) + 1e-06)).astype(jnp.bfloat16)

def project_three(normed, weights):
    flat = normed.reshape(-1, D)
    outs = []
    for index in range(3):
        outs.append(jnp.dot(flat, weights[index], preferred_element_type=jnp.float32).astype(jnp.bfloat16).reshape(normed.shape))
    return outs

def frame_attend(parts):
    query, key, value = parts
    qh = query.astype(jnp.float32).reshape(TOKS, HEADS, HEAD)
    kh = key.astype(jnp.float32).reshape(TOKS, HEADS, HEAD)
    vh = value.astype(jnp.float32).reshape(TOKS, HEADS, HEAD)
    scores = jnp.einsum('qhd,khd->hqk', qh, kh) / jnp.sqrt(jnp.float32(HEAD))
    weights = jax.nn.softmax(scores, axis=-1).astype(jnp.bfloat16)
    mixed = jnp.einsum('hqk,khd->qhd', weights.astype(jnp.float32), vh)
    return mixed.astype(jnp.bfloat16).reshape(TOKS, D)

def series_attend(parts):
    query, key, value = parts
    qh = query.astype(jnp.float32).reshape(FRAMES, HEADS, HEAD)
    kh = key.astype(jnp.float32).reshape(FRAMES, HEADS, HEAD)
    vh = value.astype(jnp.float32).reshape(FRAMES, HEADS, HEAD)
    scores = jnp.einsum('fhd,ghd->hfg', qh, kh) / jnp.sqrt(jnp.float32(HEAD))
    order = jnp.arange(FRAMES, dtype=jnp.int32)
    allowed = order[None, :] <= order[:, None]
    scores = jnp.where(allowed[None], scores, -jnp.inf)
    weights = jax.nn.softmax(scores, axis=-1)
    mixed = jnp.einsum('hfg,ghd->fhd', weights, vh)
    return mixed.astype(jnp.bfloat16).reshape(FRAMES, D)

def out_project(mixed, weight):
    return jnp.dot(mixed.reshape(-1, D), weight, preferred_element_type=jnp.float32).reshape(mixed.shape)

def reference(clip, w_spatial, w_temporal):
    normed = rms_norm(clip)
    sq, sk, sv = project_three(normed, w_spatial)
    smix = lax.map(frame_attend, (sq, sk, sv))
    after_space = (clip.astype(jnp.float32) + out_project(smix, w_spatial[3])).astype(jnp.bfloat16)
    tnormed = rms_norm(after_space)
    tq, tk, tv = project_three(tnormed, w_temporal)
    tmix = lax.map(series_attend, (jnp.swapaxes(tq, 0, 1), jnp.swapaxes(tk, 0, 1), jnp.swapaxes(tv, 0, 1)))
    tmix = jnp.swapaxes(tmix, 0, 1)
    return (after_space.astype(jnp.float32) + out_project(tmix, w_temporal[3])).astype(jnp.bfloat16)
```

```python
import math

import jax
import jax.numpy as jnp
from jax import lax
from jax.experimental import pallas as pl
from jax.experimental.pallas import tpu as pltpu
from jax.sharding import PartitionSpec as P

HEAD = 64
PAIR = 2 * HEAD
SCALE = math.log2(math.e) / math.sqrt(HEAD)
F32, BF16 = jnp.float32, jnp.bfloat16
VMEM = pl.BlockSpec(memory_space=pltpu.VMEM)


def dot(a, b):
    return jnp.dot(a, b, preferred_element_type=F32)


def rms_norm(values):
    wide = values.astype(F32)
    return (wide * lax.rsqrt(jnp.mean(wide * wide, axis=-1, keepdims=True) + 1e-06)).astype(BF16)


def halves(rows):
    first = lax.broadcasted_iota(jnp.int32, (rows, PAIR), 1) < HEAD
    one, zero = jnp.ones((rows, PAIR), F32), jnp.zeros((rows, PAIR), F32)
    return jnp.where(first, one, zero).astype(BF16), jnp.where(first, zero, one).astype(BF16)


def attend_pair(query, key, value, masks, allowed):
    rows = query.shape[0]
    low, high = masks
    both = jnp.concatenate([query * low, query * high], axis=0)
    scores = lax.dot_general(both, key, (((1,), (1,)), ((), ())), preferred_element_type=F32)
    if allowed is not None:
        scores = jnp.where(allowed, scores, -1e30)
    largest = jnp.max(scores, axis=-1, keepdims=True)
    expo = jnp.exp2((scores - largest) * SCALE).astype(BF16)
    side = jnp.concatenate([expo[:rows], expo[rows:]], axis=1)
    right = jnp.concatenate(
        [
            jnp.concatenate([value * low, low], axis=1),
            jnp.concatenate([value * high, high], axis=1),
        ],
        axis=0,
    )
    mixed = dot(side, right)
    return (mixed[:, :PAIR] / mixed[:, PAIR:]).astype(BF16)


def space_kernel(clip_ref, w_ref, out_ref, qkv_ref, mix_ref, wide_ref, send_ref):
    count, frames, toks, width = clip_ref.shape
    rows = count * toks
    groups = out_ref.shape[0]
    share = rows // groups
    masks = halves(rows)
    clip = [clip_ref[:, f].reshape(rows, width) for f in range(frames)]
    normed = jnp.concatenate([rms_norm(c) for c in clip], axis=0)
    for j in range(3):
        qkv_ref[j] = dot(normed, w_ref[j]).astype(BF16)
    for f in range(frames):
        at = pl.ds(f * rows, rows)
        for p in range(width // PAIR):
            cols = pl.ds(p * PAIR, PAIR)
            mix_ref[at, cols] = attend_pair(
                qkv_ref[0, at, cols], qkv_ref[1, at, cols], qkv_ref[2, at, cols], masks, None
            )
    out = dot(mix_ref[...], w_ref[3])
    for f in range(frames):
        after = out[f * rows : (f + 1) * rows] + clip[f].astype(F32)
        for p in range(width // PAIR):
            wide_ref[p, pl.ds(f * rows, rows), :] = after[:, p * PAIR : (p + 1) * PAIR]
    for p in range(width // PAIR):
        for f in range(frames):
            for t in range(share):
                send_ref[p, pl.ds(f * share + t, groups, stride=frames * share), :] = wide_ref[
                    p, pl.ds(f * rows + t, groups, stride=share), :
                ]
        out_ref[:, :, pl.ds(p * PAIR, PAIR)] = (
            send_ref[p].astype(BF16).reshape(groups, frames * share, PAIR)
        )


def time_kernel(x_ref, w_ref, out_ref, qkv_ref, mix_ref, wide_ref, *, toks):
    space, tm, block, width = x_ref.shape
    rows = space * tm * block
    frames = rows // toks
    pairs = width // PAIR
    masks = halves(frames)
    x = jnp.concatenate([x_ref[s, m] for m in range(tm) for s in range(space)], axis=0)
    normed = rms_norm(x)
    for j in range(3):
        out = dot(normed, w_ref[j])
        for p in range(pairs):
            qkv_ref[j, p] = out[:, p * PAIR : (p + 1) * PAIR]
    order = lax.broadcasted_iota(jnp.int32, (2 * frames, frames), 0) % frames
    allowed = lax.broadcasted_iota(jnp.int32, (2 * frames, frames), 1) <= order
    for t in range(toks):
        at = pl.ds(t, frames, stride=toks)
        for p in range(pairs):
            mix_ref[pl.ds(t * frames, frames), pl.ds(p * PAIR, PAIR)] = attend_pair(
                qkv_ref[0, p, at, :].astype(BF16),
                qkv_ref[1, p, at, :].astype(BF16),
                qkv_ref[2, p, at, :].astype(BF16),
                masks,
                allowed,
            )
    out = dot(mix_ref[...], w_ref[3])
    for p in range(pairs):
        cols = slice(p * PAIR, (p + 1) * PAIR)
        for t in range(toks):
            wide_ref[p, pl.ds(t, frames, stride=toks), :] = out[t * frames : (t + 1) * frames, cols]
        out_ref[:, pl.ds(p * PAIR, PAIR)] = (wide_ref[p] + x[:, cols].astype(F32)).astype(BF16)


def place_kernel(x_ref, out_ref, wide_ref, flat_ref):
    sources, block, width = x_ref.shape
    frames, toks, _ = out_ref.shape
    share = block // frames
    for p in range(width // PAIR):
        cols = pl.ds(p * PAIR, PAIR)
        wide_ref[p] = x_ref[:, :, cols].astype(F32).reshape(sources * block, PAIR)
        for s in range(sources):
            for t in range(share):
                flat_ref[p, pl.ds(s * share + t, frames, stride=toks), :] = wide_ref[
                    p, pl.ds(s * block + t, frames, stride=share), :
                ]
        out_ref[:, :, cols] = flat_ref[p].astype(BF16).reshape(frames, toks, PAIR)


def params():
    return pltpu.CompilerParams(vmem_limit_bytes=56 * 1024 * 1024)


def on_device(clip, w_spatial, w_temporal):
    frames, toks, width = clip.shape
    rows = frames * toks
    tm, space = lax.axis_size("tm"), lax.axis_size("space")
    share = toks // tm
    lanes = pltpu.VMEM((width // PAIR, rows, PAIR), F32)
    parts = lax.all_to_all(
        clip.reshape(space, rows // space, width), "space", split_axis=0, concat_axis=0, tiled=True
    ).reshape(space, frames // space, toks, width)
    after = pl.pallas_call(
        space_kernel,
        out_shape=jax.ShapeDtypeStruct((space * tm, rows // (space * tm), width), BF16),
        in_specs=[VMEM, VMEM],
        out_specs=VMEM,
        scratch_shapes=[
            pltpu.VMEM((3, rows, width), BF16),
            pltpu.VMEM((rows, width), BF16),
            lanes,
            lanes,
        ],
        compiler_params=params(),
        name="spatial",
    )(parts, w_spatial)
    after = lax.all_to_all(
        after, ("space", "tm"), split_axis=0, concat_axis=0, tiled=True
    )
    result = pl.pallas_call(
        lambda *refs: time_kernel(*refs, toks=share),
        out_shape=jax.ShapeDtypeStruct((rows, width), BF16),
        in_specs=[VMEM, VMEM],
        out_specs=VMEM,
        scratch_shapes=[
            pltpu.VMEM((3, width // PAIR, rows, PAIR), F32),
            pltpu.VMEM((rows, width), BF16),
            lanes,
        ],
        compiler_params=params(),
        name="temporal",
    )(after.reshape(space, tm, rows // (space * tm), width), w_temporal)
    result = lax.all_to_all(
        result.reshape(tm, rows // tm, width), "tm", split_axis=0, concat_axis=0, tiled=True
    )
    return pl.pallas_call(
        place_kernel,
        out_shape=jax.ShapeDtypeStruct((frames, toks, width), BF16),
        in_specs=[VMEM],
        out_specs=VMEM,
        scratch_shapes=[lanes, lanes],
        compiler_params=params(),
        name="place",
    )(result)


def solution(mesh):
    placed = (P("tm", "space", None), P(), P())
    return jax.shard_map(
        on_device, mesh=mesh, in_specs=placed, out_specs=P("tm", "space", None), check_vma=False
    )
```

```python
import functools
import math

import jax
import jax.numpy as jnp
from jax import lax
from jax.experimental import pallas as pl
from jax.experimental.pallas import tpu as pltpu
from jax.sharding import PartitionSpec as P

HEAD = 64
PAIR = 2 * HEAD
SCALE = math.log2(math.e) / math.sqrt(HEAD)
F32, BF16 = jnp.float32, jnp.bfloat16
MIB = 1024 * 1024


def dot(a, b):
    return jnp.dot(a, b, preferred_element_type=F32)


def rms_norm(values):
    wide = values.astype(F32)
    return (wide * lax.rsqrt(jnp.mean(wide * wide, axis=-1, keepdims=True) + 1e-06)).astype(BF16)


def halves(rows):
    first = lax.broadcasted_iota(jnp.int32, (rows, PAIR), 1) < HEAD
    one, zero = jnp.ones((rows, PAIR), F32), jnp.zeros((rows, PAIR), F32)
    return jnp.where(first, one, zero).astype(BF16), jnp.where(first, zero, one).astype(BF16)


def reorder(values, source):
    rows = values.shape[0]
    wanted = source(lax.broadcasted_iota(jnp.int32, (rows, 1), 0))
    place = lax.broadcasted_iota(jnp.int32, (rows, rows), 1)
    chosen = jnp.where(place == wanted, 1.0, 0.0).astype(BF16)
    return dot(chosen, values).astype(BF16)


def digits(number, *sizes):
    found = []
    for size in reversed(sizes):
        found.append(number & (size - 1))
        number = number >> (size.bit_length() - 1)
    return found[::-1]


def attend_pair(query, key, value, masks, allowed):
    rows = query.shape[0]
    low, high = masks
    both = jnp.concatenate([query * low, query * high], axis=0)
    scores = lax.dot_general(both, key, (((1,), (1,)), ((), ())), preferred_element_type=F32)
    if allowed is not None:
        scores = jnp.where(allowed, scores, -1e30)
    largest = jnp.max(scores, axis=-1, keepdims=True)
    expo = jnp.exp2((scores - largest) * SCALE).astype(BF16)
    side = jnp.concatenate([expo[:rows], expo[rows:]], axis=1)
    right = jnp.concatenate(
        [
            jnp.concatenate([value * low, low], axis=1),
            jnp.concatenate([value * high, high], axis=1),
        ],
        axis=0,
    )
    mixed = dot(side, right)
    return (mixed[:, :PAIR] / mixed[:, PAIR:]).astype(BF16)


def split_kernel(clip_ref, *refs):
    *out_refs, sems = refs
    me = lax.axis_index("space")
    copies = [
        pltpu.make_async_copy(clip_ref.at[me ^ k], out_ref, sems.at[k])
        for k, out_ref in enumerate(out_refs)
    ]
    for copy in copies:
        copy.start()
    for copy in copies:
        copy.wait()


def project_kernel(*refs):
    *clip_refs, w_ref, out_ref = refs
    frames, toks, width = clip_refs[0].shape
    normed = rms_norm(jnp.concatenate([c[...].reshape(-1, width) for c in clip_refs], axis=0))
    for j in range(3):
        out = dot(normed, w_ref[j]).astype(BF16)
        out_ref[j] = out.reshape(len(clip_refs), frames, toks, width)


def space_kernel(*refs, count, groups):
    clip_refs, qkv_refs, (w_ref, out_ref, mix_ref) = refs[:count], refs[count:-3], refs[-3:]
    frames, toks, width = clip_refs[0].shape
    rows = count * toks
    share = toks // groups
    block = frames * share
    masks = halves(rows)

    def part(j, f, cols):
        return jnp.concatenate(
            [ref[j, s, f, :, cols] for ref in qkv_refs for s in range(ref.shape[1])], axis=0
        )

    for f in range(frames):
        for p in range(width // PAIR):
            cols = pl.ds(p * PAIR, PAIR)
            mixed = attend_pair(part(0, f, cols), part(1, f, cols), part(2, f, cols), masks, None)
            mix_ref[pl.ds(f * rows, rows), cols] = mixed
    clip = jnp.concatenate([c[f] for f in range(frames) for c in clip_refs], axis=0)
    after = (dot(mix_ref[...], w_ref[3]) + clip.astype(F32)).astype(BF16)

    def source(row):
        k, g, f, t = digits(row, count, groups, frames, share)
        return f * rows + k * toks + g * share + t

    after = reorder(after, source).reshape(count, groups, block, width)
    me = lax.axis_index("space")
    for k in range(count):
        out_ref[pl.ds((me ^ k) * groups, groups)] = after[k]


def time_kernel(x_ref, w_ref, *refs, toks):
    *out_refs, qkv_ref, mix_ref, done_ref = refs
    groups = len(out_refs)
    space, _, block, width = x_ref.shape
    rows = space * groups * block
    frames = rows // toks
    per = block // toks
    masks = halves(frames)

    def source(row):
        t, m, s, i = digits(row, toks, groups, space, per)
        return ((s * groups + m) * per + i) * toks + t

    x = reorder(x_ref[...].reshape(rows, width), source)
    normed = rms_norm(x)
    for j in range(3):
        qkv_ref[j] = dot(normed, w_ref[j]).astype(BF16)
    order = lax.broadcasted_iota(jnp.int32, (2 * frames, frames), 0) & (frames - 1)
    allowed = lax.broadcasted_iota(jnp.int32, (2 * frames, frames), 1) <= order
    for t in range(toks):
        at = pl.ds(t * frames, frames)
        for p in range(width // PAIR):
            cols = pl.ds(p * PAIR, PAIR)
            mix_ref[at, cols] = attend_pair(
                qkv_ref[0, at, cols], qkv_ref[1, at, cols], qkv_ref[2, at, cols], masks, allowed
            )
    done_ref[...] = (dot(mix_ref[...], w_ref[3]) + x.astype(F32)).astype(BF16)
    me = lax.axis_index("tm")
    own = frames // groups
    for k, out_ref in enumerate(out_refs):
        for t in range(toks):
            at = pl.multiple_of(t * frames + (me ^ k) * own, own)
            out_ref[pl.ds(t * own, own), :] = done_ref[pl.ds(at, own), :]


def place_kernel(*refs):
    *in_refs, out_ref = refs
    frames, toks, width = out_ref.shape
    groups = len(in_refs)
    share = toks // groups
    me = lax.axis_index("tm")

    def source(row):
        f, g, t = digits(row, frames, groups, share)
        return ((g ^ me) * share + t) * frames + f

    rows = jnp.concatenate([in_ref[...] for in_ref in in_refs], axis=0)
    out_ref[...] = reorder(rows, source).reshape(out_ref.shape)


def call(kernel, name, outs, *args, scratch=(), flops=0, hbm=0, vmem=20):
    like = [jax.ShapeDtypeStruct(shape, BF16) for shape in outs]
    size = 2 * sum(math.prod(a.shape) for a in (*args, *like))
    within = pl.BlockSpec(memory_space=pltpu.VMEM)
    return pl.pallas_call(
        kernel,
        out_shape=like,
        in_specs=[pl.BlockSpec(memory_space=pl.ANY)] * hbm + [within] * (len(args) - hbm),
        out_specs=[within] * len(outs),
        scratch_shapes=scratch,
        compiler_params=pltpu.CompilerParams(vmem_limit_bytes=vmem * MIB),
        cost_estimate=pl.CostEstimate(flops=flops, bytes_accessed=size, transcendentals=0),
        name=name,
    )(*args)


def exchange(pieces, axis, order):
    count = lax.axis_size(axis)
    got = {0: pieces[0]}
    for k in order:
        got[k] = lax.ppermute(pieces[k], axis, [(i, i ^ k) for i in range(count)])
    return [got[k] for k in range(count)]


def on_device(clip, w_spatial, w_temporal):
    frames, toks, width = clip.shape
    rows = frames * toks
    tm, space = lax.axis_size("tm"), lax.axis_size("space")
    share = toks // tm
    per = frames // space
    block = per * share
    piece = (per, toks, width)
    cost = 2 * rows * width * width

    parts = call(
        split_kernel,
        "split",
        [piece] * space,
        clip.reshape(space, *piece),
        scratch=[pltpu.SemaphoreType.DMA((space,))],
        hbm=1,
        vmem=60,
    )
    parts = exchange(parts, "space", reversed(range(1, space)))
    groups = [parts[:1], parts[1:2], parts[2:]]
    qkv = [
        call(
            project_kernel,
            "project",
            [(3, len(group), *piece)],
            *group,
            w_spatial,
            flops=3 * cost * len(group) // space,
        )[0]
        for group in groups
        if group
    ]
    after = call(
        functools.partial(space_kernel, count=space, groups=tm),
        "spatial",
        [(space * tm, block, width)],
        *parts,
        *qkv,
        w_spatial,
        scratch=[pltpu.VMEM((rows, width), BF16)],
        flops=2 * cost,
    )[0]
    after = lax.all_to_all(after, ("space", "tm"), split_axis=0, concat_axis=0, tiled=True)
    result = call(
        functools.partial(time_kernel, toks=share),
        "temporal",
        [(rows // tm, width)] * tm,
        after.reshape(space, tm, block, width),
        w_temporal,
        scratch=[
            pltpu.VMEM((3, rows, width), BF16),
            pltpu.VMEM((rows, width), BF16),
            pltpu.VMEM((rows, width), BF16),
        ],
        flops=5 * cost,
    )
    order = sorted(range(1, tm), key=lambda k: (-(k >> 1).bit_count(), k & 1, k))
    result = exchange(result, "tm", order)
    return call(place_kernel, "place", [(frames, toks, width)], *result)[0]


def solution(mesh):
    placed = (P("tm", "space", None), P(), P())
    return jax.shard_map(
        on_device, mesh=mesh, in_specs=placed, out_specs=P("tm", "space", None), check_vma=False
    )
```

```python
import functools
import math

import jax
import jax.numpy as jnp
from jax import lax
from jax.experimental import pallas as pl
from jax.experimental.pallas import tpu as pltpu
from jax.sharding import PartitionSpec as P

HEAD = 64
PAIR = 2 * HEAD
SCALE = math.log2(math.e) / math.sqrt(HEAD)
F32, BF16 = jnp.float32, jnp.bfloat16
MIB = 1024 * 1024


def dot(a, b):
    return jnp.dot(a, b, preferred_element_type=F32)


def rms_norm(values):
    wide = values.astype(F32)
    return (wide * lax.rsqrt(jnp.mean(wide * wide, axis=-1, keepdims=True) + 1e-06)).astype(BF16)


def halves(rows):
    first = lax.broadcasted_iota(jnp.int32, (rows, PAIR), 1) < HEAD
    one, zero = jnp.ones((rows, PAIR), F32), jnp.zeros((rows, PAIR), F32)
    return jnp.where(first, one, zero).astype(BF16), jnp.where(first, zero, one).astype(BF16)


def reorder(values, source, rows=None, first=0):
    rows = rows or values.shape[0]
    wanted = source(lax.broadcasted_iota(jnp.int32, (rows, 1), 0) + first)
    place = lax.broadcasted_iota(jnp.int32, (rows, values.shape[0]), 1)
    chosen = jnp.where(place == wanted, 1.0, 0.0).astype(BF16)
    return dot(chosen, values).astype(BF16)


def digits(number, *sizes):
    found = []
    for size in reversed(sizes):
        found.append(number & (size - 1))
        number = number >> (size.bit_length() - 1)
    return found[::-1]


def group_of(width):
    return 2 * PAIR if width % (2 * PAIR) == 0 else PAIR


def attend(query, key, value, masks, allowed):
    rows, width = query.shape
    low, high = masks
    pairs = [slice(p, p + PAIR) for p in range(0, width, PAIR)]
    both = jnp.concatenate(
        [jnp.concatenate([query[:, p] * m for p in pairs], axis=1) for m in masks], axis=0
    )
    nothing = jnp.zeros((rows, PAIR), BF16)
    keys = jnp.concatenate(
        [
            jnp.concatenate([key[:, p] if p == q else nothing for p in pairs], axis=1)
            for q in pairs
        ],
        axis=0,
    )
    scores = lax.dot_general(both, keys, (((1,), (1,)), ((), ())), preferred_element_type=F32)
    out = []
    for i, p in enumerate(pairs):
        part = scores[:, i * rows : (i + 1) * rows]
        if allowed is not None:
            part = jnp.where(allowed, part, -1e30)
        largest = jnp.max(part, axis=-1, keepdims=True)
        expo = jnp.exp2((part - largest) * SCALE).astype(BF16)
        side = jnp.concatenate([expo[:rows], expo[rows:]], axis=1)
        right = jnp.concatenate(
            [jnp.concatenate([value[:, p] * m, m], axis=1) for m in masks], axis=0
        )
        mixed = dot(side, right)
        out.append((mixed[:, :PAIR] / mixed[:, PAIR:]).astype(BF16))
    return jnp.concatenate(out, axis=1)


def own_or_whole(clip_ref, frame):
    if len(clip_ref.shape) == 4:
        return clip_ref[lax.axis_index("space"), frame]
    return clip_ref[frame]


def project_kernel(*refs):
    *clip_refs, w_ref, out_ref = refs
    project(clip_refs, w_ref, out_ref)


def project(clip_refs, w_ref, out_ref):
    frames, toks, width = out_ref.shape[2:]
    clip = [own_or_whole(c, slice(None)).reshape(-1, width) for c in clip_refs]
    normed = rms_norm(jnp.concatenate(clip, axis=0))
    for j in range(3):
        out = dot(normed, w_ref[j]).astype(BF16)
        out_ref[j] = out.reshape(len(clip_refs), frames, toks, width)


def space_kernel(*refs, distances, groups):
    count = len(distances)
    clip_refs, refs = refs[:count], refs[count:]
    *qkv_refs, w_ref, out_ref, mix_ref, last_ref = refs
    project(clip_refs[count - last_ref.shape[1] :], w_ref, last_ref)
    qkv_refs = [*qkv_refs, last_ref]
    frames, toks, width = clip_refs[0].shape[1:]
    rows = count * toks
    share = toks // groups
    block = frames * share
    masks = halves(rows)
    group = group_of(width)

    def part(j, f, cols):
        return jnp.concatenate(
            [ref[j, s, f, :, cols] for ref in qkv_refs for s in range(ref.shape[1])], axis=0
        )

    for f in range(frames):
        for p in range(0, width, group):
            cols = pl.ds(p, group)
            mixed = attend(part(0, f, cols), part(1, f, cols), part(2, f, cols), masks, None)
            mix_ref[pl.ds(f * rows, rows), cols] = mixed
    clip = jnp.concatenate(
        [own_or_whole(c, f) for f in range(frames) for c in clip_refs], axis=0
    )
    after = (dot(mix_ref[...], w_ref[3]) + clip.astype(F32)).astype(BF16)

    def source(row):
        k, g, f, t = digits(row, count, groups, frames, share)
        return f * rows + k * toks + g * share + t

    after = reorder(after, source).reshape(count, groups, block, width)
    me = lax.axis_index("space")
    for i, k in enumerate(distances):
        out_ref[pl.ds((me ^ k) * groups, groups)] = after[i]


def time_kernel(x_ref, w_ref, *refs, toks, last):
    *out_refs, qkv_ref, mix_ref, done_ref = refs
    space, groups, block, width = x_ref.shape
    rows = space * groups * block
    frames = rows // toks
    per = block // toks
    masks = halves(frames)
    group = group_of(width)

    def source(row):
        t, m, s, i = digits(row, toks, groups, space, per)
        return ((s * groups + m) * per + i) * toks + t

    x = reorder(x_ref[...].reshape(rows, width), source)
    normed = rms_norm(x)
    for j in range(3):
        qkv_ref[j] = dot(normed, w_ref[j]).astype(BF16)
    order = lax.broadcasted_iota(jnp.int32, (2 * frames, frames), 0) & (frames - 1)
    allowed = lax.broadcasted_iota(jnp.int32, (2 * frames, frames), 1) <= order
    for t in range(toks):
        at = pl.ds(t * frames, frames)
        for p in range(0, width, group):
            cols = pl.ds(p, group)
            mix_ref[at, cols] = attend(
                qkv_ref[0, at, cols], qkv_ref[1, at, cols], qkv_ref[2, at, cols], masks, allowed
            )
    done_ref[...] = (dot(mix_ref[...], w_ref[3]) + x.astype(F32)).astype(BF16)
    me = lax.axis_index("tm")
    own = frames // groups
    for k in range(groups):
        for t in range(toks):
            at = pl.multiple_of(t * frames + (me ^ k) * own, own)
            block = done_ref[pl.ds(at, own), :]
            if k // 2 == last:
                out_refs[groups // 2 - 1 + k % 2][pl.ds(t * own, own), :] = block
            else:
                out_refs[k // 2 - (k // 2 > last)][k % 2, pl.ds(t * own, own), :] = block


def place_kernel(*refs, order, groups, toks):
    *in_refs, out_ref = refs
    frames, _, width = in_refs[-1].shape[0] * groups // toks, 0, in_refs[-1].shape[1]
    steps = frames // out_ref.shape[0]
    share = toks // groups
    far = groups // 2
    me = lax.axis_index("tm")
    first = pl.program_id(0) * (frames // steps * toks)

    def source(row):
        f, g, t = digits(row, frames, groups, share)
        return ((g ^ me) * share + t) * frames + f

    pairs = {k: (in_refs[i].at[0], in_refs[far - 1 + i]) for i, k in enumerate(order[:-1])}
    pairs[order[-1]] = in_refs[-2:]
    rows = jnp.concatenate([part[...] for k in range(far) for part in pairs[k]], axis=0)
    done = reorder(rows, source, frames // steps * toks, first)
    out_ref[...] = done.reshape(out_ref.shape)


def call(kernel, name, outs, *args, scratch=(), flops=0, **blocks):
    like = [jax.ShapeDtypeStruct(shape, BF16) for shape in outs]
    size = 2 * sum(math.prod(a.shape) for a in (*args, *like))
    within = pl.BlockSpec(memory_space=pltpu.VMEM)
    return pl.pallas_call(
        kernel,
        out_shape=like,
        in_specs=[within] * len(args),
        out_specs=blocks.pop("out_specs", [within] * len(outs)),
        scratch_shapes=scratch,
        compiler_params=pltpu.CompilerParams(vmem_limit_bytes=20 * MIB),
        cost_estimate=pl.CostEstimate(flops=flops, bytes_accessed=size, transcendentals=0),
        name=name,
        **blocks,
    )(*args)


def exchange(pieces, axis, order, unit=1):
    count = lax.axis_size(axis)
    got = {0: pieces[0]}
    for k in order:
        got[k] = lax.ppermute(pieces[k], axis, [(i, i ^ (k * unit)) for i in range(count)])
    return [got[k] for k in range(len(pieces))]


def on_device(clip, w_spatial, w_temporal):
    frames, toks, width = clip.shape
    rows = frames * toks
    tm, space = lax.axis_size("tm"), lax.axis_size("space")
    share = toks // tm
    per = frames // space
    block = per * share
    piece = (per, toks, width)
    cost = 2 * rows * width * width

    blocks = clip.reshape(space, *piece)
    me = lax.axis_index("space")
    parts = [blocks] + [
        lax.dynamic_index_in_dim(blocks, me ^ k, 0, keepdims=False) for k in range(1, space)
    ]
    parts = exchange(parts, "space", sorted(range(1, space), key=lambda k: (k == 1, k)))
    groups = [[0], [2], [1], [*range(3, space)]] if space > 3 else [[*range(space)]]
    qkv = [
        call(
            project_kernel,
            "project",
            [(3, len(group), *piece)],
            *[parts[k] for k in group],
            w_spatial,
            flops=3 * cost * len(group) // space,
        )[0]
        for group in groups[:-1]
    ]
    after = call(
        functools.partial(space_kernel, distances=sum(groups, []), groups=tm),
        "spatial",
        [(space * tm, block, width)],
        *[parts[k] for k in sum(groups, [])],
        *qkv,
        w_spatial,
        scratch=[
            pltpu.VMEM((rows, width), BF16),
            pltpu.VMEM((3, len(groups[-1]), *piece), BF16),
        ],
        flops=2 * cost,
    )[0]
    after = lax.all_to_all(after, ("space", "tm"), split_axis=0, concat_axis=0, tiled=True)
    order = [0, *sorted(range(1, tm // 2), key=lambda k: (-k.bit_count(), k))]
    result = call(
        functools.partial(time_kernel, toks=share, last=order[-1]),
        "temporal",
        [(2, rows // tm, width)] * (tm // 2 - 1) + [(rows // tm, width)] * 2,
        after.reshape(space, tm, block, width),
        w_temporal,
        scratch=[
            pltpu.VMEM((3, rows, width), BF16),
            pltpu.VMEM((rows, width), BF16),
            pltpu.VMEM((rows, width), BF16),
        ],
        flops=5 * cost,
    )
    last = order[-1]
    direct = [
        lax.ppermute(part, "tm", [(i, i ^ (2 * last + s)) for i in range(tm)])
        for s, part in enumerate(result[-2:])
    ]
    whole = dict(zip([k for k in range(tm // 2) if k != last], result))
    whole = {
        k: lax.ppermute(part, "tm", [(i, i ^ (2 * k)) for i in range(tm)]) if k else part
        for k, part in whole.items()
    }
    beside = {
        k: lax.ppermute(part[1], "tm", [(i, i ^ 1) for i in range(tm)])
        for k, part in whole.items()
    }
    steps = 2 if frames % 2 == 0 else 1
    return call(
        functools.partial(place_kernel, order=order, groups=tm, toks=toks),
        "place",
        [(frames, toks, width)],
        *[whole[k] for k in order[:-1]],
        *[beside[k] for k in order[:-1]],
        *direct,
        grid=(steps,),
        out_specs=[pl.BlockSpec((frames // steps, toks, width), lambda i: (i, 0, 0))],
    )[0]


def solution(mesh):
    placed = (P("tm", "space", None), P(), P())
    return jax.shard_map(
        on_device, mesh=mesh, in_specs=placed, out_specs=P("tm", "space", None), check_vma=False
    )
```

```python
import functools
import math

import jax
import jax.numpy as jnp
from jax import lax
from jax.experimental import pallas as pl
from jax.experimental.pallas import tpu as pltpu
from jax.sharding import PartitionSpec as P

HEAD = 64
PAIR = 2 * HEAD
SCALE = math.log2(math.e) / math.sqrt(HEAD)
F32, BF16 = jnp.float32, jnp.bfloat16
MIB = 1024 * 1024


def dot(a, b):
    return jnp.dot(a, b, preferred_element_type=F32)


def rms_norm(values):
    wide = values.astype(F32)
    return (wide * lax.rsqrt(jnp.mean(wide * wide, axis=-1, keepdims=True) + 1e-06)).astype(BF16)


def halves(rows):
    first = lax.broadcasted_iota(jnp.int32, (rows, PAIR), 1) < HEAD
    one, zero = jnp.ones((rows, PAIR), F32), jnp.zeros((rows, PAIR), F32)
    return jnp.where(first, one, zero).astype(BF16), jnp.where(first, zero, one).astype(BF16)


def digits(number, *sizes):
    found = []
    for size in reversed(sizes):
        found.append(number & (size - 1))
        number = number >> (size.bit_length() - 1)
    return found[::-1]


def orders(rows, *, count, groups, share):
    toks, frames = groups * share, rows // (groups * share)
    per = frames // count

    def leave_space(row):
        k, g, f, t = digits(row, count, groups, per, share)
        return f * count * toks + k * toks + g * share + t

    def enter_time(row):
        t, m, s, i = digits(row, share, groups, count, per)
        return ((s * groups + m) * per + i) * share + t

    def leave_time(row, me):
        f, g, t = digits(row, frames, groups, share)
        return ((g ^ me) * share + t) * frames + f

    return leave_space, enter_time, leave_time


def table_kernel(_, *out_refs, **sizes):
    rows = out_refs[0].shape[0]
    leave_space, enter_time, leave_time = orders(rows, **sizes)
    me = lax.axis_index("tm")
    row = lax.broadcasted_iota(jnp.int32, (rows, 1), 0)
    place = lax.broadcasted_iota(jnp.int32, (rows, rows), 1)
    wanted = [leave_space(row), enter_time(row), leave_time(row, me)]
    for out_ref, source in zip(out_refs, wanted):
        out_ref[...] = jnp.where(place == source, 1.0, 0.0).astype(BF16)


def group_of(width):
    return 2 * PAIR if width % (2 * PAIR) == 0 else PAIR


def attend(query, key, value, masks, allowed):
    rows, width = query.shape
    low, high = masks
    pairs = [slice(p, p + PAIR) for p in range(0, width, PAIR)]
    both = jnp.concatenate(
        [jnp.concatenate([query[:, p] * m for p in pairs], axis=1) for m in masks], axis=0
    )
    nothing = jnp.zeros((rows, PAIR), BF16)
    keys = jnp.concatenate(
        [
            jnp.concatenate([key[:, p] if p == q else nothing for p in pairs], axis=1)
            for q in pairs
        ],
        axis=0,
    )
    scores = lax.dot_general(both, keys, (((1,), (1,)), ((), ())), preferred_element_type=F32)
    out = []
    for i, p in enumerate(pairs):
        part = scores[:, i * rows : (i + 1) * rows]
        if allowed is not None:
            part = jnp.where(allowed, part, -1e30)
        largest = jnp.max(part, axis=-1, keepdims=True)
        expo = jnp.exp2((part - largest) * SCALE).astype(BF16)
        side = jnp.concatenate([expo[:rows], expo[rows:]], axis=1)
        right = jnp.concatenate(
            [jnp.concatenate([value[:, p] * m, m], axis=1) for m in masks], axis=0
        )
        mixed = dot(side, right)
        out.append((mixed[:, :PAIR] / mixed[:, PAIR:]).astype(BF16))
    return jnp.concatenate(out, axis=1)


def own_or_whole(clip_ref, frame):
    if len(clip_ref.shape) == 4:
        return clip_ref[lax.axis_index("space"), frame]
    return clip_ref[frame]


def project_kernel(*refs):
    *clip_refs, w_ref, out_ref = refs
    project(clip_refs, w_ref, out_ref)


def project(clip_refs, w_ref, out_ref):
    frames, toks, width = out_ref.shape[2:]
    clip = [own_or_whole(c, slice(None)).reshape(-1, width) for c in clip_refs]
    normed = rms_norm(jnp.concatenate(clip, axis=0))
    for j in range(3):
        out = dot(normed, w_ref[j]).astype(BF16)
        out_ref[j] = out.reshape(len(clip_refs), frames, toks, width)


def space_kernel(*refs, distances, groups):
    count = len(distances)
    clip_refs, refs = refs[:count], refs[count:]
    *qkv_refs, w_ref, order_ref, out_ref, mix_ref, last_ref = refs
    project(clip_refs[count - last_ref.shape[1] :], w_ref, last_ref)
    qkv_refs = [*qkv_refs, last_ref]
    frames, toks, width = clip_refs[0].shape[1:]
    rows = count * toks
    share = toks // groups
    block = frames * share
    masks = halves(rows)
    group = group_of(width)

    def part(j, f, cols):
        return jnp.concatenate(
            [ref[j, s, f, :, cols] for ref in qkv_refs for s in range(ref.shape[1])], axis=0
        )

    for f in range(frames):
        for p in range(0, width, group):
            cols = pl.ds(p, group)
            mixed = attend(part(0, f, cols), part(1, f, cols), part(2, f, cols), masks, None)
            mix_ref[pl.ds(f * rows, rows), cols] = mixed
    clip = jnp.concatenate(
        [own_or_whole(c, f) for f in range(frames) for c in clip_refs], axis=0
    )
    after = (dot(mix_ref[...], w_ref[3]) + clip.astype(F32)).astype(BF16)
    after = dot(order_ref[...], after).astype(BF16).reshape(count, groups, block, width)
    me = lax.axis_index("space")
    for i, k in enumerate(distances):
        out_ref[pl.ds((me ^ k) * groups, groups)] = after[i]


def time_kernel(x_ref, w_ref, order_ref, *refs, toks, both, direct):
    *out_refs, qkv_ref, mix_ref, done_ref = refs
    space, groups, block, width = x_ref.shape
    rows = space * groups * block
    frames = rows // toks
    masks = halves(frames)
    group = group_of(width)

    x = dot(order_ref[...], x_ref[...].reshape(rows, width)).astype(BF16)
    normed = rms_norm(x)
    for j in range(3):
        qkv_ref[j] = dot(normed, w_ref[j]).astype(BF16)
    order = lax.broadcasted_iota(jnp.int32, (2 * frames, frames), 0) & (frames - 1)
    allowed = lax.broadcasted_iota(jnp.int32, (2 * frames, frames), 1) <= order
    for t in range(toks):
        at = pl.ds(t * frames, frames)
        for p in range(0, width, group):
            cols = pl.ds(p, group)
            mix_ref[at, cols] = attend(
                qkv_ref[0, at, cols], qkv_ref[1, at, cols], qkv_ref[2, at, cols], masks, allowed
            )
    done_ref[...] = (dot(mix_ref[...], w_ref[3]) + x.astype(F32)).astype(BF16)
    me = lax.axis_index("tm")
    own = frames // groups
    for k in range(groups):
        for t in range(toks):
            at = pl.multiple_of(t * frames + (me ^ k) * own, own)
            block = done_ref[pl.ds(at, own), :]
            if k // 2 in both:
                out_refs[both.index(k // 2)][k % 2, pl.ds(t * own, own), :] = block
            else:
                out_refs[len(both) + direct.index(k)][pl.ds(t * own, own), :] = block


def place_kernel(*refs, both, direct):
    *in_refs, order_ref, out_ref, done_ref, sems = refs
    frames, toks, width = out_ref.shape
    parts = {2 * k: in_refs[i].at[0] for i, k in enumerate(both)}
    parts |= {2 * k + 1: in_refs[len(both) + i] for i, k in enumerate(both)}
    parts |= {k: in_refs[2 * len(both) + i] for i, k in enumerate(direct)}
    rows = jnp.concatenate([parts[k][...] for k in range(len(parts))], axis=0)
    steps = sems.shape[0]
    some = frames // steps
    copies = []
    for step in range(steps):
        at = pl.ds(step * some, some)
        done = dot(order_ref[pl.ds(step * some * toks, some * toks), :], rows).astype(BF16)
        done_ref[at] = done.reshape(some, toks, width)
        copies.append(pltpu.make_async_copy(done_ref.at[at], out_ref.at[at], sems.at[step]))
        copies[-1].start()
    for copy in copies:
        copy.wait()


def call(kernel, name, outs, *args, scratch=(), flops=0, **blocks):
    like = [jax.ShapeDtypeStruct(shape, BF16) for shape in outs]
    size = 2 * sum(math.prod(a.shape) for a in (*args, *like))
    within = pl.BlockSpec(memory_space=pltpu.VMEM)
    return pl.pallas_call(
        kernel,
        out_shape=like,
        in_specs=[within] * len(args),
        out_specs=blocks.pop("out_specs", [within] * len(outs)),
        scratch_shapes=scratch,
        compiler_params=pltpu.CompilerParams(vmem_limit_bytes=20 * MIB),
        cost_estimate=pl.CostEstimate(flops=flops, bytes_accessed=size, transcendentals=0),
        name=name,
        **blocks,
    )(*args)


def exchange(pieces, axis, order, unit=1):
    count = lax.axis_size(axis)
    got = {0: pieces[0]}
    for k in order:
        got[k] = lax.ppermute(pieces[k], axis, [(i, i ^ (k * unit)) for i in range(count)])
    return [got[k] for k in range(len(pieces))]


def on_device(clip, w_spatial, w_temporal):
    frames, toks, width = clip.shape
    rows = frames * toks
    tm, space = lax.axis_size("tm"), lax.axis_size("space")
    share = toks // tm
    per = frames // space
    block = per * share
    piece = (per, toks, width)
    cost = 2 * rows * width * width

    blocks = clip.reshape(space, *piece)
    me = lax.axis_index("space")
    near = sorted(range(1, space), key=lambda k: (k == 1, k))
    parts = {0: blocks}
    held = blocks
    for k in near:
        parts[k] = lax.dynamic_index_in_dim(held, me ^ k, 0, keepdims=False)
        held = lax.optimization_barrier((blocks, parts[k]))[0]
    parts = [parts[k] for k in range(space)]
    parts = exchange(parts, "space", sorted(range(1, space), key=lambda k: (k == 1, k)))
    groups = [[0], [2], [1], [*range(3, space)]] if space > 3 else [[*range(space)]]
    qkv = [
        call(
            project_kernel,
            "project",
            [(3, len(group), *piece)],
            *[parts[k] for k in group],
            w_spatial,
            flops=3 * cost * len(group) // space,
        )[0]
        for group in groups[:-1]
    ]
    leave_space, enter_time, leave_time = call(
        functools.partial(
            table_kernel, count=space, groups=tm, share=share
        ),
        "orders",
        [(rows, rows)] * 3,
        qkv[0] if qkv else parts[0],
    )
    after = call(
        functools.partial(space_kernel, distances=sum(groups, []), groups=tm),
        "spatial",
        [(space * tm, block, width)],
        *[parts[k] for k in sum(groups, [])],
        *qkv,
        w_spatial,
        leave_space,
        scratch=[
            pltpu.VMEM((rows, width), BF16),
            pltpu.VMEM((3, len(groups[-1]), *piece), BF16),
        ],
        flops=2 * cost,
    )[0]
    after = lax.all_to_all(after, ("space", "tm"), split_axis=0, concat_axis=0, tiled=True)
    both = [k for k in range(tm // 2) if k.bit_count() != 1]
    direct = [2 * k + s for s in range(2) for k in reversed(range(tm // 2)) if k not in both]
    result = call(
        functools.partial(time_kernel, toks=share, both=both, direct=direct),
        "temporal",
        [(2, rows // tm, width)] * len(both) + [(rows // tm, width)] * len(direct),
        after.reshape(space, tm, block, width),
        w_temporal,
        enter_time,
        scratch=[
            pltpu.VMEM((3, rows, width), BF16),
            pltpu.VMEM((rows, width), BF16),
            pltpu.VMEM((rows, width), BF16),
        ],
        flops=5 * cost,
    )

    def over_tm(part, distance):
        return lax.ppermute(part, "tm", [(i, i ^ distance) for i in range(tm)])

    whole = [over_tm(part, 2 * k) if k else part for k, part in zip(both, result)]
    beside = [over_tm(part[1], 1) for part in whole]
    near = [over_tm(part, k) for k, part in zip(direct, result[len(both) :])]
    steps = 4 if frames % 4 == 0 else 1
    return call(
        functools.partial(place_kernel, both=both, direct=direct),
        "place",
        [(frames, toks, width)],
        *whole,
        *beside,
        *near,
        leave_time,
        out_specs=[pl.BlockSpec(memory_space=pl.ANY)],
        scratch=[
            pltpu.VMEM((frames, toks, width), BF16),
            pltpu.SemaphoreType.DMA((steps,)),
        ],
    )[0]


def solution(mesh):
    placed = (P("tm", "space", None), P(), P())
    return jax.shard_map(
        on_device, mesh=mesh, in_specs=placed, out_specs=P("tm", "space", None), check_vma=False
    )
```

```python
import functools
import math

import jax
import jax.numpy as jnp
from jax import lax
from jax.experimental import pallas as pl
from jax.experimental.pallas import tpu as pltpu
from jax.sharding import PartitionSpec as P

HEAD = 64
PAIR = 2 * HEAD
SCALE = math.log2(math.e) / math.sqrt(HEAD)
F32, BF16 = jnp.float32, jnp.bfloat16
MIB = 1024 * 1024


def dot(a, b):
    return jnp.dot(a, b, preferred_element_type=F32)


def rms_norm(values):
    wide = values.astype(F32)
    return (wide * lax.rsqrt(jnp.mean(wide * wide, axis=-1, keepdims=True) + 1e-06)).astype(BF16)


def halves(rows):
    first = lax.broadcasted_iota(jnp.int32, (rows, PAIR), 1) < HEAD
    one, zero = jnp.ones((rows, PAIR), F32), jnp.zeros((rows, PAIR), F32)
    return jnp.where(first, one, zero).astype(BF16), jnp.where(first, zero, one).astype(BF16)


def digits(number, *sizes):
    found = []
    for size in reversed(sizes):
        found.append(number & (size - 1))
        number = number >> (size.bit_length() - 1)
    return found[::-1]


def orders(rows, *, count, groups, share):
    toks, frames = groups * share, rows // (groups * share)
    per = frames // count

    def leave_space(row):
        k, g, f, t = digits(row, count, groups, per, share)
        return f * count * toks + k * toks + g * share + t

    def enter_time(row):
        t, m, s, i = digits(row, share, groups, count, per)
        return ((s * groups + m) * per + i) * share + t

    def leave_time(row, me):
        f, g, t = digits(row, frames, groups, share)
        return ((g ^ me) * share + t) * frames + f

    return leave_space, enter_time, leave_time


def table_kernel(_, *out_refs, **sizes):
    some, rows = out_refs[0].shape[0], out_refs[1].shape[0]
    leave_space, _, _ = orders(some, **sizes)
    _, enter_time, leave_time = orders(rows, **sizes)
    me = lax.axis_index("tm")
    for out_ref, source in zip(out_refs, (leave_space, enter_time, lambda r: leave_time(r, me))):
        shape = out_ref.shape
        wanted = source(lax.broadcasted_iota(jnp.int32, (shape[0], 1), 0))
        place = lax.broadcasted_iota(jnp.int32, shape, 1)
        out_ref[...] = jnp.where(place == wanted, 1.0, 0.0).astype(BF16)


def group_of(width):
    return 2 * PAIR if width % (2 * PAIR) == 0 else PAIR


def attend(query, key, value, masks, allowed):
    rows, width = query.shape
    low, high = masks
    pairs = [slice(p, p + PAIR) for p in range(0, width, PAIR)]
    both = jnp.concatenate(
        [jnp.concatenate([query[:, p] * m for p in pairs], axis=1) for m in masks], axis=0
    )
    nothing = jnp.zeros((rows, PAIR), BF16)
    keys = jnp.concatenate(
        [
            jnp.concatenate([key[:, p] if p == q else nothing for p in pairs], axis=1)
            for q in pairs
        ],
        axis=0,
    )
    scores = lax.dot_general(both, keys, (((1,), (1,)), ((), ())), preferred_element_type=F32)
    out = []
    for i, p in enumerate(pairs):
        part = scores[:, i * rows : (i + 1) * rows]
        if allowed is not None:
            part = jnp.where(allowed, part, -1e30)
        largest = jnp.max(part, axis=-1, keepdims=True)
        expo = jnp.exp2((part - largest) * SCALE).astype(BF16)
        side = jnp.concatenate([expo[:rows], expo[rows:]], axis=1)
        right = jnp.concatenate(
            [jnp.concatenate([value[:, p] * m, m], axis=1) for m in masks], axis=0
        )
        mixed = dot(side, right)
        out.append((mixed[:, :PAIR] / mixed[:, PAIR:]).astype(BF16))
    return jnp.concatenate(out, axis=1)


def own_or_whole(clip_ref, frame):
    if len(clip_ref.shape) == 4:
        return clip_ref[lax.axis_index("space"), frame]
    return clip_ref[frame]


def project_kernel(*refs):
    *clip_refs, w_ref, out_ref = refs
    project(clip_refs, w_ref, out_ref)


def project(clip_refs, w_ref, out_ref):
    frames, toks, width = out_ref.shape[2:]
    clip = [own_or_whole(c, slice(None)).reshape(-1, width) for c in clip_refs]
    normed = rms_norm(jnp.concatenate(clip, axis=0))
    for j in range(3):
        out = dot(normed, w_ref[j]).astype(BF16)
        out_ref[j] = out.reshape(len(clip_refs), frames, toks, width)


def space_kernel(*refs, distances, late, groups, first):
    count = len(distances)
    clip_refs, refs = refs[:count], refs[count:]
    *refs, w_ref, order_ref, out_ref, mix_ref, last_ref = refs
    qkv_refs, before = (refs[:-1], refs[-1]) if first else (refs, None)
    project(clip_refs[count - late :], w_ref, last_ref)
    frames, toks, width = last_ref.shape[2:]
    rows = count * toks
    share = toks // groups
    masks = halves(rows)
    group = group_of(width)

    def part(j, f, cols):
        early = [ref[j, s, first + f, :, cols] for ref in qkv_refs for s in range(ref.shape[1])]
        return jnp.concatenate(early + [last_ref[j, s, f, :, cols] for s in range(late)], axis=0)

    for f in range(frames):
        for p in range(0, width, group):
            cols = pl.ds(p, group)
            mixed = attend(part(0, f, cols), part(1, f, cols), part(2, f, cols), masks, None)
            mix_ref[pl.ds(f * rows, rows), cols] = mixed
    clip = [
        own_or_whole(c, f if i >= count - late else first + f)
        for f in range(frames)
        for i, c in enumerate(clip_refs)
    ]
    after = dot(mix_ref[...], w_ref[3]) + jnp.concatenate(clip, axis=0).astype(F32)
    after = dot(order_ref[...], after.astype(BF16)).astype(BF16)
    after = after.reshape(count, groups, frames * share, width)
    me = lax.axis_index("space")
    for i, k in enumerate(distances):
        at = pl.ds((me ^ k) * groups, groups)
        if before is None:
            out_ref[at] = after[i]
        else:
            out_ref[at] = jnp.concatenate([before[at], after[i]], axis=1)


def time_kernel(x_ref, w_ref, order_ref, *refs, toks, both, direct):
    *out_refs, qkv_ref, mix_ref, done_ref = refs
    space, groups, block, width = x_ref.shape
    rows = space * groups * block
    frames = rows // toks
    masks = halves(frames)
    group = group_of(width)

    x = dot(order_ref[...], x_ref[...].reshape(rows, width)).astype(BF16)
    normed = rms_norm(x)
    for j in range(3):
        qkv_ref[j] = dot(normed, w_ref[j]).astype(BF16)
    order = lax.broadcasted_iota(jnp.int32, (2 * frames, frames), 0) & (frames - 1)
    allowed = lax.broadcasted_iota(jnp.int32, (2 * frames, frames), 1) <= order
    for t in range(toks):
        at = pl.ds(t * frames, frames)
        for p in range(0, width, group):
            cols = pl.ds(p, group)
            mix_ref[at, cols] = attend(
                qkv_ref[0, at, cols], qkv_ref[1, at, cols], qkv_ref[2, at, cols], masks, allowed
            )
    done_ref[...] = (dot(mix_ref[...], w_ref[3]) + x.astype(F32)).astype(BF16)
    me = lax.axis_index("tm")
    own = frames // groups
    for k in range(groups):
        for t in range(toks):
            at = pl.multiple_of(t * frames + (me ^ k) * own, own)
            block = done_ref[pl.ds(at, own), :]
            if k // 2 in both:
                out_refs[both.index(k // 2)][k % 2, pl.ds(t * own, own), :] = block
            else:
                out_refs[len(both) + direct.index(k)][pl.ds(t * own, own), :] = block


def place_kernel(*refs, both, direct):
    *in_refs, order_ref, out_ref, done_ref, sems = refs
    frames, toks, width = out_ref.shape
    parts = {2 * k: in_refs[i].at[0] for i, k in enumerate(both)}
    parts |= {2 * k + 1: in_refs[len(both) + i] for i, k in enumerate(both)}
    parts |= {k: in_refs[2 * len(both) + i] for i, k in enumerate(direct)}
    rows = jnp.concatenate([parts[k][...] for k in range(len(parts))], axis=0)
    steps = sems.shape[0]
    some = frames // steps
    copies = []
    for step in range(steps):
        at = pl.ds(step * some, some)
        done = dot(order_ref[pl.ds(step * some * toks, some * toks), :], rows).astype(BF16)
        done_ref[at] = done.reshape(some, toks, width)
        copies.append(pltpu.make_async_copy(done_ref.at[at], out_ref.at[at], sems.at[step]))
        copies[-1].start()
    for copy in copies:
        copy.wait()


def call(kernel, name, outs, *args, scratch=(), flops=0, **blocks):
    like = [jax.ShapeDtypeStruct(shape, BF16) for shape in outs]
    size = 2 * sum(math.prod(a.shape) for a in (*args, *like))
    within = pl.BlockSpec(memory_space=pltpu.VMEM)
    return pl.pallas_call(
        kernel,
        out_shape=like,
        in_specs=[within] * len(args),
        out_specs=blocks.pop("out_specs", [within] * len(outs)),
        scratch_shapes=scratch,
        compiler_params=pltpu.CompilerParams(vmem_limit_bytes=20 * MIB),
        cost_estimate=pl.CostEstimate(flops=flops, bytes_accessed=size, transcendentals=0),
        name=name,
        **blocks,
    )(*args)


def on_device(clip, w_spatial, w_temporal):
    frames, toks, width = clip.shape
    rows = frames * toks
    tm, space = lax.axis_size("tm"), lax.axis_size("space")
    share = toks // tm
    per = frames // space
    block = per * share
    piece = (per, toks, width)
    cost = 2 * rows * width * width

    blocks = clip.reshape(space, *piece)
    me = lax.axis_index("space")
    early = [0, 2, 1] if space > 3 else [0]
    late = [k for k in range(space) if k not in early]
    chunks = 2 if per % 2 == 0 and late else 1
    step = per // chunks
    parts = {0: blocks}
    held = blocks
    for k in early[1:] + late:
        parts[k] = lax.dynamic_index_in_dim(held, me ^ k, 0, keepdims=False)
        held = lax.optimization_barrier((blocks, parts[k]))[0]

    def over_space(part, distance):
        return lax.ppermute(part, "space", [(i, i ^ distance) for i in range(space)])

    for k in early[1:]:
        parts[k] = over_space(parts[k], k)
    ends = [
        [over_space(parts[k][c * step : (c + 1) * step], k) for k in late] for c in range(chunks)
    ]
    groups = [[k] for k in early]
    qkv = [
        call(
            project_kernel,
            "project",
            [(3, len(group), *piece)],
            *[parts[k] for k in group],
            w_spatial,
            flops=3 * cost * len(group) // space,
        )[0]
        for group in groups
    ]
    leave_space, enter_time, leave_time = call(
        functools.partial(
            table_kernel, count=space, groups=tm, share=share
        ),
        "orders",
        [(rows // chunks, rows // chunks), (rows, rows), (rows, rows)],
        qkv[0],
    )
    before = []
    for c in range(chunks):
        before = call(
            functools.partial(
                space_kernel, distances=early + late, late=len(late), groups=tm, first=c * step
            ),
            "spatial",
            [(space * tm, (c + 1) * step * share, width)],
            *[parts[k] for k in early],
            *ends[c],
            *qkv,
            *before,
            w_spatial,
            leave_space,
            scratch=[
                pltpu.VMEM((rows // chunks, width), BF16),
                pltpu.VMEM((3, len(late), step, toks, width), BF16),
            ],
            flops=2 * cost // chunks,
        )
    after = before[0]
    after = lax.all_to_all(after, ("space", "tm"), split_axis=0, concat_axis=0, tiled=True)
    both = [k for k in range(tm // 2) if k.bit_count() != 1]
    direct = [2 * k + s for s in range(2) for k in reversed(range(tm // 2)) if k not in both]
    result = call(
        functools.partial(time_kernel, toks=share, both=both, direct=direct),
        "temporal",
        [(2, rows // tm, width)] * len(both) + [(rows // tm, width)] * len(direct),
        after.reshape(space, tm, block, width),
        w_temporal,
        enter_time,
        scratch=[
            pltpu.VMEM((3, rows, width), BF16),
            pltpu.VMEM((rows, width), BF16),
            pltpu.VMEM((rows, width), BF16),
        ],
        flops=5 * cost,
    )

    def over_tm(part, distance):
        return lax.ppermute(part, "tm", [(i, i ^ distance) for i in range(tm)])

    whole = [over_tm(part, 2 * k) if k else part for k, part in zip(both, result)]
    beside = [over_tm(part[1], 1) for part in whole]
    near = [over_tm(part, k) for k, part in zip(direct, result[len(both) :])]
    steps = 4 if frames % 4 == 0 else 1
    return call(
        functools.partial(place_kernel, both=both, direct=direct),
        "place",
        [(frames, toks, width)],
        *whole,
        *beside,
        *near,
        leave_time,
        out_specs=[pl.BlockSpec(memory_space=pl.ANY)],
        scratch=[
            pltpu.VMEM((frames, toks, width), BF16),
            pltpu.SemaphoreType.DMA((steps,)),
        ],
    )[0]


def solution(mesh):
    placed = (P("tm", "space", None), P(), P())
    return jax.shard_map(
        on_device, mesh=mesh, in_specs=placed, out_specs=P("tm", "space", None), check_vma=False
    )
```

```python
import functools
import math

import jax
import jax.numpy as jnp
from jax import lax
from jax.experimental import pallas as pl
from jax.experimental.pallas import tpu as pltpu
from jax.sharding import PartitionSpec as P

HEAD = 64
PAIR = 2 * HEAD
SCALE = math.log2(math.e) / math.sqrt(HEAD)
F32, BF16 = jnp.float32, jnp.bfloat16
MIB = 1024 * 1024


def dot(a, b):
    return jnp.dot(a, b, preferred_element_type=F32)


def rms_norm(values):
    wide = values.astype(F32)
    return (wide * lax.rsqrt(jnp.mean(wide * wide, axis=-1, keepdims=True) + 1e-06)).astype(BF16)


def halves(rows):
    first = lax.broadcasted_iota(jnp.int32, (rows, PAIR), 1) < HEAD
    one, zero = jnp.ones((rows, PAIR), F32), jnp.zeros((rows, PAIR), F32)
    return jnp.where(first, one, zero).astype(BF16), jnp.where(first, zero, one).astype(BF16)


def digits(number, *sizes):
    found = []
    for size in reversed(sizes):
        found.append(number & (size - 1))
        number = number >> (size.bit_length() - 1)
    return found[::-1]


def orders(rows, *, count, groups, share):
    toks, frames = groups * share, rows // (groups * share)
    per = frames // count

    def leave_space(row):
        k, g, f, t = digits(row, count, groups, per, share)
        return f * count * toks + k * toks + g * share + t

    def enter_time(row):
        t, m, s, i = digits(row, share, groups, count, per)
        return ((s * groups + m) * per + i) * share + t

    def leave_time(row, me):
        f, g, t = digits(row, frames, groups, share)
        return ((g ^ me) * share + t) * frames + f

    return leave_space, enter_time, leave_time


def table_kernel(_, *out_refs, **sizes):
    some, rows = out_refs[0].shape[0], out_refs[1].shape[0]
    leave_space, _, _ = orders(some, **sizes)
    _, enter_time, leave_time = orders(rows, **sizes)
    me = lax.axis_index("tm")
    for out_ref, source in zip(out_refs, (leave_space, enter_time, lambda r: leave_time(r, me))):
        shape = out_ref.shape
        wanted = source(lax.broadcasted_iota(jnp.int32, (shape[0], 1), 0))
        place = lax.broadcasted_iota(jnp.int32, shape, 1)
        out_ref[...] = jnp.where(place == wanted, 1.0, 0.0).astype(BF16)


def group_of(width):
    return 2 * PAIR if width % (2 * PAIR) == 0 else PAIR


def attend(query, key, value, masks, allowed):
    rows, width = query.shape
    low, high = masks
    pairs = [slice(p, p + PAIR) for p in range(0, width, PAIR)]
    both = jnp.concatenate(
        [jnp.concatenate([query[:, p] * m for p in pairs], axis=1) for m in masks], axis=0
    )
    nothing = jnp.zeros((rows, PAIR), BF16)
    keys = jnp.concatenate(
        [
            jnp.concatenate([key[:, p] if p == q else nothing for p in pairs], axis=1)
            for q in pairs
        ],
        axis=0,
    )
    scores = lax.dot_general(both, keys, (((1,), (1,)), ((), ())), preferred_element_type=F32)
    out = []
    for i, p in enumerate(pairs):
        part = scores[:, i * rows : (i + 1) * rows]
        if allowed is not None:
            part = jnp.where(allowed, part, -1e30)
        largest = jnp.max(part, axis=-1, keepdims=True)
        expo = jnp.exp2((part - largest) * SCALE).astype(BF16)
        side = jnp.concatenate([expo[:rows], expo[rows:]], axis=1)
        right = jnp.concatenate(
            [jnp.concatenate([value[:, p] * m, m], axis=1) for m in masks], axis=0
        )
        mixed = dot(side, right)
        out.append((mixed[:, :PAIR] / mixed[:, PAIR:]).astype(BF16))
    return jnp.concatenate(out, axis=1)


def own_or_whole(clip_ref, frame):
    if len(clip_ref.shape) == 4:
        return clip_ref[lax.axis_index("space"), frame]
    return clip_ref[frame]


def project_kernel(*refs):
    *clip_refs, w_ref, out_ref = refs
    project(clip_refs, w_ref, out_ref)


def project(clip_refs, w_ref, out_ref):
    frames, toks, width = out_ref.shape[2:]
    clip = [own_or_whole(c, slice(None)).reshape(-1, width) for c in clip_refs]
    normed = rms_norm(jnp.concatenate(clip, axis=0))
    for j in range(3):
        out = dot(normed, w_ref[j]).astype(BF16)
        out_ref[j] = out.reshape(len(clip_refs), frames, toks, width)


def space_kernel(*refs, distances, late, groups, first):
    count = len(distances)
    clip_refs, refs = refs[:count], refs[count:]
    *refs, w_ref, order_ref, out_ref, mix_ref, last_ref = refs
    qkv_refs, before = (refs[:-1], refs[-1]) if first else (refs, None)
    project(clip_refs[count - late :], w_ref, last_ref)
    frames, toks, width = last_ref.shape[2:]
    rows = count * toks
    share = toks // groups
    masks = halves(rows)
    group = group_of(width)

    def part(j, f, cols):
        early = [ref[j, s, first + f, :, cols] for ref in qkv_refs for s in range(ref.shape[1])]
        return jnp.concatenate(early + [last_ref[j, s, f, :, cols] for s in range(late)], axis=0)

    for f in range(frames):
        for p in range(0, width, group):
            cols = pl.ds(p, group)
            mixed = attend(part(0, f, cols), part(1, f, cols), part(2, f, cols), masks, None)
            mix_ref[pl.ds(f * rows, rows), cols] = mixed
    clip = [
        own_or_whole(c, f if i >= count - late else first + f)
        for f in range(frames)
        for i, c in enumerate(clip_refs)
    ]
    after = dot(mix_ref[...], w_ref[3]) + jnp.concatenate(clip, axis=0).astype(F32)
    after = dot(order_ref[...], after.astype(BF16)).astype(BF16)
    after = after.reshape(count, groups, frames * share, width)
    me = lax.axis_index("space")
    for i, k in enumerate(distances):
        at = pl.ds((me ^ k) * groups, groups)
        if before is None:
            out_ref[at] = after[i]
        else:
            out_ref[at] = jnp.concatenate([before[at], after[i]], axis=1)


def time_kernel(x_ref, w_ref, order_ref, *refs, toks, both, direct):
    *out_refs, qkv_ref, mix_ref, done_ref = refs
    space, groups, block, width = x_ref.shape
    rows = space * groups * block
    frames = rows // toks
    masks = halves(frames)
    group = group_of(width)

    x = dot(order_ref[...], x_ref[...].reshape(rows, width)).astype(BF16)
    normed = rms_norm(x)
    for j in range(3):
        qkv_ref[j] = dot(normed, w_ref[j]).astype(BF16)
    order = lax.broadcasted_iota(jnp.int32, (2 * frames, frames), 0) & (frames - 1)
    allowed = lax.broadcasted_iota(jnp.int32, (2 * frames, frames), 1) <= order
    for t in range(toks):
        at = pl.ds(t * frames, frames)
        for p in range(0, width, group):
            cols = pl.ds(p, group)
            mix_ref[at, cols] = attend(
                qkv_ref[0, at, cols], qkv_ref[1, at, cols], qkv_ref[2, at, cols], masks, allowed
            )
    done_ref[...] = (dot(mix_ref[...], w_ref[3]) + x.astype(F32)).astype(BF16)
    me = lax.axis_index("tm")
    own = frames // groups
    for k in range(groups):
        for t in range(toks):
            at = pl.multiple_of(t * frames + (me ^ k) * own, own)
            block = done_ref[pl.ds(at, own), :]
            if k // 2 in both:
                out_refs[both.index(k // 2)][k % 2, pl.ds(t * own, own), :] = block
            else:
                out_refs[len(both) + direct.index(k)][pl.ds(t * own, own), :] = block


def place_kernel(*refs, both, direct):
    *in_refs, order_ref, out_ref, done_ref, sems = refs
    frames, toks, width = out_ref.shape
    parts = {2 * k: in_refs[i].at[0] for i, k in enumerate(both)}
    parts |= {2 * k + 1: in_refs[len(both) + i] for i, k in enumerate(both)}
    parts[1] = parts[1].at[1 - lax.axis_index("tm") % 2]
    parts |= {k: in_refs[2 * len(both) + i] for i, k in enumerate(direct)}
    rows = jnp.concatenate([parts[k][...] for k in range(len(parts))], axis=0)
    steps = sems.shape[0]
    some = frames // steps
    copies = []
    for step in range(steps):
        at = pl.ds(step * some, some)
        done = dot(order_ref[pl.ds(step * some * toks, some * toks), :], rows).astype(BF16)
        done_ref[at] = done.reshape(some, toks, width)
        copies.append(pltpu.make_async_copy(done_ref.at[at], out_ref.at[at], sems.at[step]))
        copies[-1].start()
    for copy in copies:
        copy.wait()


def call(kernel, name, outs, *args, scratch=(), flops=0, **blocks):
    like = [jax.ShapeDtypeStruct(shape, BF16) for shape in outs]
    size = 2 * sum(math.prod(a.shape) for a in (*args, *like))
    within = pl.BlockSpec(memory_space=pltpu.VMEM)
    return pl.pallas_call(
        kernel,
        out_shape=like,
        in_specs=[within] * len(args),
        out_specs=blocks.pop("out_specs", [within] * len(outs)),
        scratch_shapes=scratch,
        compiler_params=pltpu.CompilerParams(vmem_limit_bytes=20 * MIB),
        cost_estimate=pl.CostEstimate(flops=flops, bytes_accessed=size, transcendentals=0),
        name=name,
        **blocks,
    )(*args)


def on_device(clip, w_spatial, w_temporal):
    frames, toks, width = clip.shape
    rows = frames * toks
    tm, space = lax.axis_size("tm"), lax.axis_size("space")
    share = toks // tm
    per = frames // space
    block = per * share
    piece = (per, toks, width)
    cost = 2 * rows * width * width

    blocks = clip.reshape(space, *piece)
    me = lax.axis_index("space")
    early = [0, 2, 1] if space > 3 else [0]
    late = [k for k in range(space) if k not in early]
    chunks = 2 if per % 2 == 0 and late else 1
    step = per // chunks
    parts = {0: blocks}
    held = blocks
    for k in early[1:] + late:
        parts[k] = lax.dynamic_index_in_dim(held, me ^ k, 0, keepdims=False)
        held = lax.optimization_barrier((blocks, parts[k]))[0]

    def over_space(part, distance):
        return lax.ppermute(part, "space", [(i, i ^ distance) for i in range(space)])

    for k in early[1:]:
        parts[k] = over_space(parts[k], k)
    ends = [
        [over_space(parts[k][c * step : (c + 1) * step], k) for k in late] for c in range(chunks)
    ]
    groups = [[k] for k in early]
    qkv = [
        call(
            project_kernel,
            "project",
            [(3, len(group), *piece)],
            *[parts[k] for k in group],
            w_spatial,
            flops=3 * cost * len(group) // space,
        )[0]
        for group in groups
    ]
    leave_space, enter_time, leave_time = call(
        functools.partial(
            table_kernel, count=space, groups=tm, share=share
        ),
        "orders",
        [(rows // chunks, rows // chunks), (rows, rows), (rows, rows)],
        qkv[0],
    )
    before = []
    for c in range(chunks):
        before = call(
            functools.partial(
                space_kernel, distances=early + late, late=len(late), groups=tm, first=c * step
            ),
            "spatial",
            [(space * tm, (c + 1) * step * share, width)],
            *[parts[k] for k in early],
            *ends[c],
            *qkv,
            *before,
            w_spatial,
            leave_space,
            scratch=[
                pltpu.VMEM((rows // chunks, width), BF16),
                pltpu.VMEM((3, len(late), step, toks, width), BF16),
            ],
            flops=2 * cost // chunks,
        )
    after = before[0]
    after = lax.all_to_all(after, ("space", "tm"), split_axis=0, concat_axis=0, tiled=True)
    both = [k for k in range(tm // 2) if k.bit_count() != 1]
    direct = [2 * k + s for s in range(2) for k in reversed(range(tm // 2)) if k not in both]
    result = call(
        functools.partial(time_kernel, toks=share, both=both, direct=direct),
        "temporal",
        [(2, rows // tm, width)] * len(both) + [(rows // tm, width)] * len(direct),
        after.reshape(space, tm, block, width),
        w_temporal,
        enter_time,
        scratch=[
            pltpu.VMEM((3, rows, width), BF16),
            pltpu.VMEM((rows, width), BF16),
            pltpu.VMEM((rows, width), BF16),
        ],
        flops=5 * cost,
    )

    def over_tm(part, distance):
        return lax.ppermute(part, "tm", [(i, i ^ distance) for i in range(tm)])

    whole = [over_tm(part, 2 * k) if k else part for k, part in zip(both, result)]
    pairs = [[i, i + 1] for i in range(0, tm, 2)]
    beside = [lax.all_gather(whole[0][1], "tm", axis_index_groups=pairs)]
    beside += [over_tm(part[1], 1) for part in whole[1:]]
    near = [over_tm(part, k) for k, part in zip(direct, result[len(both) :])]
    steps = 4 if frames % 4 == 0 else 1
    return call(
        functools.partial(place_kernel, both=both, direct=direct),
        "place",
        [(frames, toks, width)],
        *whole,
        *beside,
        *near,
        leave_time,
        out_specs=[pl.BlockSpec(memory_space=pl.ANY)],
        scratch=[
            pltpu.VMEM((frames, toks, width), BF16),
            pltpu.SemaphoreType.DMA((steps,)),
        ],
    )[0]


def solution(mesh):
    placed = (P("tm", "space", None), P(), P())
    return jax.shard_map(
        on_device, mesh=mesh, in_specs=placed, out_specs=P("tm", "space", None), check_vma=False
    )
```

```python
import functools
import math

import jax
import jax.numpy as jnp
from jax import lax
from jax.experimental import pallas as pl
from jax.experimental.pallas import tpu as pltpu
from jax.sharding import PartitionSpec as P

HEAD = 64
PAIR = 2 * HEAD
SCALE = math.log2(math.e) / math.sqrt(HEAD)
F32, BF16 = jnp.float32, jnp.bfloat16
MIB = 1024 * 1024


def dot(a, b):
    return jnp.dot(a, b, preferred_element_type=F32)


def rms_norm(values):
    wide = values.astype(F32)
    return (wide * lax.rsqrt(jnp.mean(wide * wide, axis=-1, keepdims=True) + 1e-06)).astype(BF16)


def halves(rows):
    first = lax.broadcasted_iota(jnp.int32, (rows, PAIR), 1) < HEAD
    one, zero = jnp.ones((rows, PAIR), F32), jnp.zeros((rows, PAIR), F32)
    return jnp.where(first, one, zero).astype(BF16), jnp.where(first, zero, one).astype(BF16)


def digits(number, *sizes):
    found = []
    for size in reversed(sizes):
        found.append(number & (size - 1))
        number = number >> (size.bit_length() - 1)
    return found[::-1]


def orders(rows, *, count, groups, share):
    toks, frames = groups * share, rows // (groups * share)
    per = frames // count

    def leave_space(row):
        k, g, f, t = digits(row, count, groups, per, share)
        return f * count * toks + k * toks + g * share + t

    def enter_time(row):
        t, m, s, i = digits(row, share, groups, count, per)
        return ((s * groups + m) * per + i) * share + t

    def leave_time(row, me):
        f, g, t = digits(row, frames, groups, share)
        return ((g ^ me) * share + t) * frames + f

    return leave_space, enter_time, leave_time


def table_kernel(_, *out_refs, **sizes):
    some, rows = out_refs[0].shape[0], out_refs[1].shape[0]
    leave_space, _, _ = orders(some, **sizes)
    _, enter_time, leave_time = orders(rows, **sizes)
    me = lax.axis_index("tm")
    for out_ref, source in zip(out_refs, (leave_space, enter_time, lambda r: leave_time(r, me))):
        shape = out_ref.shape
        wanted = source(lax.broadcasted_iota(jnp.int32, (shape[0], 1), 0))
        place = lax.broadcasted_iota(jnp.int32, shape, 1)
        out_ref[...] = jnp.where(place == wanted, 1.0, 0.0).astype(BF16)


def group_of(width):
    return 2 * PAIR if width % (2 * PAIR) == 0 else PAIR


def attend(query, key, value, masks, allowed):
    rows, width = query.shape
    low, high = masks
    pairs = [slice(p, p + PAIR) for p in range(0, width, PAIR)]
    both = jnp.concatenate(
        [jnp.concatenate([query[:, p] * m for p in pairs], axis=1) for m in masks], axis=0
    )
    nothing = jnp.zeros((rows, PAIR), BF16)
    keys = jnp.concatenate(
        [
            jnp.concatenate([key[:, p] if p == q else nothing for p in pairs], axis=1)
            for q in pairs
        ],
        axis=0,
    )
    scores = lax.dot_general(both, keys, (((1,), (1,)), ((), ())), preferred_element_type=F32)
    out = []
    for i, p in enumerate(pairs):
        part = scores[:, i * rows : (i + 1) * rows]
        if allowed is not None:
            part = jnp.where(allowed, part, -1e30)
        largest = jnp.max(part, axis=-1, keepdims=True)
        expo = jnp.exp2((part - largest) * SCALE).astype(BF16)
        side = jnp.concatenate([expo[:rows], expo[rows:]], axis=1)
        right = jnp.concatenate(
            [jnp.concatenate([value[:, p] * m, m], axis=1) for m in masks], axis=0
        )
        mixed = dot(side, right)
        out.append((mixed[:, :PAIR] / mixed[:, PAIR:]).astype(BF16))
    return jnp.concatenate(out, axis=1)


def own_or_whole(clip_ref, frame):
    if len(clip_ref.shape) == 4:
        return clip_ref[lax.axis_index("space"), frame]
    return clip_ref[frame]


def project_kernel(*refs):
    *clip_refs, w_ref, out_ref = refs
    project(clip_refs, w_ref, out_ref)


def project(clip_refs, w_ref, out_ref):
    frames, toks, width = out_ref.shape[2:]
    clip = [own_or_whole(c, slice(None)).reshape(-1, width) for c in clip_refs]
    normed = rms_norm(jnp.concatenate(clip, axis=0))
    for j in range(3):
        out = dot(normed, w_ref[j]).astype(BF16)
        out_ref[j] = out.reshape(len(clip_refs), frames, toks, width)


def space_kernel(*refs, distances, late, groups, first):
    count = len(distances)
    clip_refs, refs = refs[:count], refs[count:]
    *refs, w_ref, order_ref, out_ref, mix_ref, last_ref = refs
    qkv_refs, before = (refs[:-1], refs[-1]) if first else (refs, None)
    project(clip_refs[count - late :], w_ref, last_ref)
    frames, toks, width = last_ref.shape[2:]
    rows = count * toks
    share = toks // groups
    masks = halves(rows)
    group = group_of(width)

    def part(j, f, cols):
        early = [ref[j, s, first + f, :, cols] for ref in qkv_refs for s in range(ref.shape[1])]
        return jnp.concatenate(early + [last_ref[j, s, f, :, cols] for s in range(late)], axis=0)

    for f in range(frames):
        for p in range(0, width, group):
            cols = pl.ds(p, group)
            mixed = attend(part(0, f, cols), part(1, f, cols), part(2, f, cols), masks, None)
            mix_ref[pl.ds(f * rows, rows), cols] = mixed
    clip = [
        own_or_whole(c, f if i >= count - late else first + f)
        for f in range(frames)
        for i, c in enumerate(clip_refs)
    ]
    after = dot(mix_ref[...], w_ref[3]) + jnp.concatenate(clip, axis=0).astype(F32)
    after = dot(order_ref[...], after.astype(BF16)).astype(BF16)
    after = after.reshape(count, groups, frames * share, width)
    me = lax.axis_index("space")
    for i, k in enumerate(distances):
        at = pl.ds((me ^ k) * groups, groups)
        if before is None:
            out_ref[at] = after[i]
        else:
            out_ref[at] = jnp.concatenate([before[at], after[i]], axis=1)


def time_kernel(x_ref, w_ref, order_ref, *refs, toks, both, direct):
    *out_refs, qkv_ref, mix_ref, done_ref = refs
    space, groups, block, width = x_ref.shape
    rows = space * groups * block
    frames = rows // toks
    masks = halves(frames)
    group = group_of(width)

    x = dot(order_ref[...], x_ref[...].reshape(rows, width)).astype(BF16)
    normed = rms_norm(x)
    for j in range(3):
        qkv_ref[j] = dot(normed, w_ref[j]).astype(BF16)
    order = lax.broadcasted_iota(jnp.int32, (2 * frames, frames), 0) & (frames - 1)
    allowed = lax.broadcasted_iota(jnp.int32, (2 * frames, frames), 1) <= order
    for t in range(toks):
        at = pl.ds(t * frames, frames)
        for p in range(0, width, group):
            cols = pl.ds(p, group)
            mix_ref[at, cols] = attend(
                qkv_ref[0, at, cols], qkv_ref[1, at, cols], qkv_ref[2, at, cols], masks, allowed
            )
    done_ref[...] = (dot(mix_ref[...], w_ref[3]) + x.astype(F32)).astype(BF16)
    me = lax.axis_index("tm")
    own = frames // groups
    for k in range(groups):
        for t in range(toks):
            at = pl.multiple_of(t * frames + (me ^ k) * own, own)
            block = done_ref[pl.ds(at, own), :]
            if k // 2 in both:
                out_refs[both.index(k // 2)][k % 2, pl.ds(t * own, own), :] = block
            else:
                out_refs[len(both) + direct.index(k)][pl.ds(t * own, own), :] = block


def place_kernel(*refs, both, direct):
    *in_refs, order_ref, out_ref, done_ref, sems = refs
    frames, toks, width = out_ref.shape
    parts = {2 * k: in_refs[i].at[0] for i, k in enumerate(both)}
    parts |= {2 * k + 1: in_refs[len(both) + i] for i, k in enumerate(both)}
    parts[1] = parts[1].at[1 - lax.axis_index("tm") % 2]
    parts |= {k: in_refs[2 * len(both) + i] for i, k in enumerate(direct)}
    rows = jnp.concatenate([parts[k][...] for k in range(len(parts))], axis=0)
    steps = sems.shape[0]
    some = frames // steps
    copies = []
    for step in range(steps):
        at = pl.ds(step * some, some)
        done = dot(order_ref[pl.ds(step * some * toks, some * toks), :], rows).astype(BF16)
        done_ref[at] = done.reshape(some, toks, width)
        copies.append(pltpu.make_async_copy(done_ref.at[at], out_ref.at[at], sems.at[step]))
        copies[-1].start()
    for copy in copies:
        copy.wait()


def call(kernel, name, outs, *args, scratch=(), flops=0, **blocks):
    like = [jax.ShapeDtypeStruct(shape, BF16) for shape in outs]
    size = 2 * sum(math.prod(a.shape) for a in (*args, *like))
    within = pl.BlockSpec(memory_space=pltpu.VMEM)
    return pl.pallas_call(
        kernel,
        out_shape=like,
        in_specs=[within] * len(args),
        out_specs=blocks.pop("out_specs", [within] * len(outs)),
        scratch_shapes=scratch,
        compiler_params=pltpu.CompilerParams(vmem_limit_bytes=20 * MIB),
        cost_estimate=pl.CostEstimate(flops=flops, bytes_accessed=size, transcendentals=0),
        name=name,
        **blocks,
    )(*args)


def on_device(clip, w_spatial, w_temporal):
    frames, toks, width = clip.shape
    rows = frames * toks
    tm, space = lax.axis_size("tm"), lax.axis_size("space")
    share = toks // tm
    per = frames // space
    block = per * share
    piece = (per, toks, width)
    cost = 2 * rows * width * width

    blocks = clip.reshape(space, *piece)
    me = lax.axis_index("space")
    early = [0, 2, 1] if space > 3 else [0]
    late = [k for k in range(space) if k not in early]
    chunks = 2 if per % 2 == 0 and late else 1
    step = per // chunks
    parts = {0: blocks}
    held = blocks
    for k in early[1:] + late:
        parts[k] = lax.dynamic_index_in_dim(held, me ^ k, 0, keepdims=False)
        held = lax.optimization_barrier((blocks, parts[k]))[0]

    def over_space(part, distance):
        return lax.ppermute(part, "space", [(i, i ^ distance) for i in range(space)])

    for k in early[1:]:
        parts[k] = over_space(parts[k], k)
    ends = [
        [over_space(parts[k][c * step : (c + 1) * step], k) for k in late] for c in range(chunks)
    ]
    groups = [[k] for k in early]
    qkv = [
        call(
            project_kernel,
            "project",
            [(3, len(group), *piece)],
            *[parts[k] for k in group],
            w_spatial,
            flops=3 * cost * len(group) // space,
        )[0]
        for group in groups
    ]
    leave_space, enter_time, leave_time = call(
        functools.partial(
            table_kernel, count=space, groups=tm, share=share
        ),
        "orders",
        [(rows // chunks, rows // chunks), (rows, rows), (rows, rows)],
        qkv[0],
    )
    before = []
    for c in range(chunks):
        before = call(
            functools.partial(
                space_kernel, distances=early + late, late=len(late), groups=tm, first=c * step
            ),
            "spatial",
            [(space * tm, (c + 1) * step * share, width)],
            *[parts[k] for k in early],
            *ends[c],
            *qkv,
            *before,
            w_spatial,
            leave_space,
            scratch=[
                pltpu.VMEM((rows // chunks, width), BF16),
                pltpu.VMEM((3, len(late), step, toks, width), BF16),
            ],
            flops=2 * cost // chunks,
        )
    after = before[0]
    after = lax.all_to_all(after, ("space", "tm"), split_axis=0, concat_axis=0, tiled=True)
    both = [k for k in range(tm // 2) if k.bit_count() != 1]
    direct = [2 * k + s for s in range(2) for k in range(tm // 2) if k not in both]
    result = call(
        functools.partial(time_kernel, toks=share, both=both, direct=direct),
        "temporal",
        [(2, rows // tm, width)] * len(both) + [(rows // tm, width)] * len(direct),
        after.reshape(space, tm, block, width),
        w_temporal,
        enter_time,
        scratch=[
            pltpu.VMEM((3, rows, width), BF16),
            pltpu.VMEM((rows, width), BF16),
            pltpu.VMEM((rows, width), BF16),
        ],
        flops=5 * cost,
    )

    def over_tm(part, distance):
        return lax.ppermute(part, "tm", [(i, i ^ distance) for i in range(tm)])

    whole = [over_tm(part, 2 * k) if k else part for k, part in zip(both, result)]
    pairs = [[i, i + 1] for i in range(0, tm, 2)]
    beside = [lax.all_gather(whole[0][1], "tm", axis_index_groups=pairs)]
    beside += [over_tm(part[1], 1) for part in whole[1:]]
    near = [over_tm(part, k) for k, part in zip(direct, result[len(both) :])]
    steps = 4 if frames % 4 == 0 else 1
    return call(
        functools.partial(place_kernel, both=both, direct=direct),
        "place",
        [(frames, toks, width)],
        *whole,
        *beside,
        *near,
        leave_time,
        out_specs=[pl.BlockSpec(memory_space=pl.ANY)],
        scratch=[
            pltpu.VMEM((frames, toks, width), BF16),
            pltpu.SemaphoreType.DMA((steps,)),
        ],
    )[0]


def solution(mesh):
    placed = (P("tm", "space", None), P(), P())
    return jax.shard_map(
        on_device, mesh=mesh, in_specs=placed, out_specs=P("tm", "space", None), check_vma=False
    )
```

```python
import functools
import math

import jax
import jax.numpy as jnp
from jax import lax
from jax.experimental import pallas as pl
from jax.experimental.pallas import tpu as pltpu
from jax.sharding import PartitionSpec as P

HEAD = 64
PAIR = 2 * HEAD
SCALE = math.log2(math.e) / math.sqrt(HEAD)
F32, BF16 = jnp.float32, jnp.bfloat16
MIB = 1024 * 1024


def dot(a, b):
    return jnp.dot(a, b, preferred_element_type=F32)


def rms_norm(values):
    wide = values.astype(F32)
    return (wide * lax.rsqrt(jnp.mean(wide * wide, axis=-1, keepdims=True) + 1e-06)).astype(BF16)


def halves(rows):
    first = lax.broadcasted_iota(jnp.int32, (rows, PAIR), 1) < HEAD
    one, zero = jnp.ones((rows, PAIR), F32), jnp.zeros((rows, PAIR), F32)
    return jnp.where(first, one, zero).astype(BF16), jnp.where(first, zero, one).astype(BF16)


def digits(number, *sizes):
    found = []
    for size in reversed(sizes):
        found.append(number & (size - 1))
        number = number >> (size.bit_length() - 1)
    return found[::-1]


def orders(rows, *, count, groups, share):
    toks, frames = groups * share, rows // (groups * share)
    per = frames // count

    def leave_space(row):
        k, g, f, t = digits(row, count, groups, per, share)
        return f * count * toks + k * toks + g * share + t

    def enter_time(row):
        t, m, s, i = digits(row, share, groups, count, per)
        return ((s * groups + m) * per + i) * share + t

    def leave_time(row, me):
        f, g, t = digits(row, frames, groups, share)
        return ((g ^ me) * share + t) * frames + f

    return leave_space, enter_time, leave_time


def table_kernel(_, *out_refs, **sizes):
    leave_space, enter_time, leave_time = orders(out_refs[0].shape[0], **sizes)
    me = lax.axis_index("tm")
    for out_ref, source in zip(out_refs, (leave_space, enter_time, lambda r: leave_time(r, me))):
        shape = out_ref.shape
        wanted = source(lax.broadcasted_iota(jnp.int32, (shape[0], 1), 0))
        place = lax.broadcasted_iota(jnp.int32, shape, 1)
        out_ref[...] = jnp.where(place == wanted, 1.0, 0.0).astype(BF16)


def group_of(width):
    return 2 * PAIR if width % (2 * PAIR) == 0 else PAIR


def attend(query, key, value, masks, allowed):
    rows, width = query.shape
    low, high = masks
    pairs = [slice(p, p + PAIR) for p in range(0, width, PAIR)]
    both = jnp.concatenate(
        [jnp.concatenate([query[:, p] * m for p in pairs], axis=1) for m in masks], axis=0
    )
    nothing = jnp.zeros((rows, PAIR), BF16)
    keys = jnp.concatenate(
        [
            jnp.concatenate([key[:, p] if p == q else nothing for p in pairs], axis=1)
            for q in pairs
        ],
        axis=0,
    )
    scores = lax.dot_general(both, keys, (((1,), (1,)), ((), ())), preferred_element_type=F32)
    out = []
    for i, p in enumerate(pairs):
        part = scores[:, i * rows : (i + 1) * rows]
        if allowed is not None:
            part = jnp.where(allowed, part, -1e30)
        largest = jnp.max(part, axis=-1, keepdims=True)
        expo = jnp.exp2((part - largest) * SCALE).astype(BF16)
        side = jnp.concatenate([expo[:rows], expo[rows:]], axis=1)
        right = jnp.concatenate(
            [jnp.concatenate([value[:, p] * m, m], axis=1) for m in masks], axis=0
        )
        mixed = dot(side, right)
        out.append((mixed[:, :PAIR] / mixed[:, PAIR:]).astype(BF16))
    return jnp.concatenate(out, axis=1)


def own_or_whole(clip_ref, frame):
    if len(clip_ref.shape) == 4:
        return clip_ref[lax.axis_index("space"), frame]
    return clip_ref[frame]


def project_kernel(*refs):
    *clip_refs, w_ref, out_ref = refs
    project(clip_refs, w_ref, out_ref)


def project(clip_refs, w_ref, out_ref):
    frames, toks, width = out_ref.shape[2:]
    clip = [own_or_whole(c, slice(None)).reshape(-1, width) for c in clip_refs]
    normed = rms_norm(jnp.concatenate(clip, axis=0))
    for j in range(3):
        out = dot(normed, w_ref[j]).astype(BF16)
        out_ref[j] = out.reshape(len(clip_refs), frames, toks, width)


def space_kernel(*refs, distances, late, groups, first):
    count = len(distances)
    clip_refs, refs = refs[:count], refs[count:]
    *refs, w_ref, order_ref, out_ref, mix_ref, last_ref = refs
    qkv_refs, before = (refs[:-1], refs[-1]) if first else (refs, None)
    project(clip_refs[count - late :], w_ref, last_ref)
    frames, toks, width = last_ref.shape[2:]
    rows = count * toks
    share = toks // groups
    masks = halves(rows)
    group = group_of(width)

    def part(j, f, cols):
        early = [ref[j, s, first + f, :, cols] for ref in qkv_refs for s in range(ref.shape[1])]
        return jnp.concatenate(early + [last_ref[j, s, f, :, cols] for s in range(late)], axis=0)

    for f in range(frames):
        for p in range(0, width, group):
            cols = pl.ds(p, group)
            mixed = attend(part(0, f, cols), part(1, f, cols), part(2, f, cols), masks, None)
            mix_ref[pl.ds(f * rows, rows), cols] = mixed
    clip = [
        own_or_whole(c, f if i >= count - late else first + f)
        for f in range(frames)
        for i, c in enumerate(clip_refs)
    ]
    after = dot(mix_ref[...], w_ref[3]) + jnp.concatenate(clip, axis=0).astype(F32)
    after = after.astype(BF16)
    if len(out_ref.shape) == 2:
        out_ref[...] = after
        return
    if before is not None:
        after = jnp.concatenate([before[...], after], axis=0)
    after = dot(order_ref[...], after).astype(BF16).reshape(count, groups, -1, width)
    me = lax.axis_index("space")
    for i, k in enumerate(distances):
        out_ref[pl.ds((me ^ k) * groups, groups)] = after[i]


def time_kernel(x_ref, w_ref, order_ref, *refs, toks, both, direct):
    *out_refs, qkv_ref, mix_ref, done_ref = refs
    space, groups, block, width = x_ref.shape
    rows = space * groups * block
    frames = rows // toks
    masks = halves(frames)
    group = group_of(width)

    x = dot(order_ref[...], x_ref[...].reshape(rows, width)).astype(BF16)
    normed = rms_norm(x)
    for j in range(3):
        qkv_ref[j] = dot(normed, w_ref[j]).astype(BF16)
    order = lax.broadcasted_iota(jnp.int32, (2 * frames, frames), 0) & (frames - 1)
    allowed = lax.broadcasted_iota(jnp.int32, (2 * frames, frames), 1) <= order
    for t in range(toks):
        at = pl.ds(t * frames, frames)
        for p in range(0, width, group):
            cols = pl.ds(p, group)
            mix_ref[at, cols] = attend(
                qkv_ref[0, at, cols], qkv_ref[1, at, cols], qkv_ref[2, at, cols], masks, allowed
            )
    done_ref[...] = (dot(mix_ref[...], w_ref[3]) + x.astype(F32)).astype(BF16)
    me = lax.axis_index("tm")
    own = frames // groups
    for k in range(groups):
        for t in range(toks):
            at = pl.multiple_of(t * frames + (me ^ k) * own, own)
            block = done_ref[pl.ds(at, own), :]
            if k // 2 in both:
                out_refs[both.index(k // 2)][k % 2, pl.ds(t * own, own), :] = block
            else:
                out_refs[len(both) + direct.index(k)][pl.ds(t * own, own), :] = block


def place_kernel(*refs, both, direct):
    *in_refs, order_ref, out_ref, done_ref, sems = refs
    frames, toks, width = out_ref.shape
    parts = {2 * k: in_refs[i].at[0] for i, k in enumerate(both)}
    parts |= {2 * k + 1: in_refs[len(both) + i] for i, k in enumerate(both)}
    parts[1] = parts[1].at[1 - lax.axis_index("tm") % 2]
    parts |= {k: in_refs[2 * len(both) + i] for i, k in enumerate(direct)}
    rows = jnp.concatenate([parts[k][...] for k in range(len(parts))], axis=0)
    steps = sems.shape[0]
    some = frames // steps
    copies = []
    for step in range(steps):
        at = pl.ds(step * some, some)
        done = dot(order_ref[pl.ds(step * some * toks, some * toks), :], rows).astype(BF16)
        done_ref[at] = done.reshape(some, toks, width)
        copies.append(pltpu.make_async_copy(done_ref.at[at], out_ref.at[at], sems.at[step]))
        copies[-1].start()
    for copy in copies:
        copy.wait()


def call(kernel, name, outs, *args, scratch=(), flops=0, **blocks):
    like = [jax.ShapeDtypeStruct(shape, BF16) for shape in outs]
    size = 2 * sum(math.prod(a.shape) for a in (*args, *like))
    within = pl.BlockSpec(memory_space=pltpu.VMEM)
    return pl.pallas_call(
        kernel,
        out_shape=like,
        in_specs=[within] * len(args),
        out_specs=blocks.pop("out_specs", [within] * len(outs)),
        scratch_shapes=scratch,
        compiler_params=pltpu.CompilerParams(vmem_limit_bytes=20 * MIB),
        cost_estimate=pl.CostEstimate(flops=flops, bytes_accessed=size, transcendentals=0),
        name=name,
        **blocks,
    )(*args)


def on_device(clip, w_spatial, w_temporal):
    frames, toks, width = clip.shape
    rows = frames * toks
    tm, space = lax.axis_size("tm"), lax.axis_size("space")
    share = toks // tm
    per = frames // space
    block = per * share
    piece = (per, toks, width)
    cost = 2 * rows * width * width

    blocks = clip.reshape(space, *piece)
    me = lax.axis_index("space")
    early = [0, 2, 1] if space > 3 else [0]
    late = [k for k in range(space) if k not in early]
    chunks = 2 if per % 2 == 0 and late else 1
    step = per // chunks
    parts = {0: blocks}
    held = blocks
    for k in early[1:] + late:
        parts[k] = lax.dynamic_index_in_dim(held, me ^ k, 0, keepdims=False)
        held = lax.optimization_barrier((blocks, parts[k]))[0]

    def over_space(part, distance):
        return lax.ppermute(part, "space", [(i, i ^ distance) for i in range(space)])

    for k in early[1:]:
        parts[k] = over_space(parts[k], k)
    ends = [
        [over_space(parts[k][c * step : (c + 1) * step], k) for k in late] for c in range(chunks)
    ]
    groups = [[k] for k in early]
    qkv = [
        call(
            project_kernel,
            "project",
            [(3, len(group), *piece)],
            *[parts[k] for k in group],
            w_spatial,
            flops=3 * cost * len(group) // space,
        )[0]
        for group in groups
    ]
    leave_space, enter_time, leave_time = call(
        functools.partial(
            table_kernel, count=space, groups=tm, share=share
        ),
        "orders",
        [(rows, rows)] * 3,
        qkv[0],
    )
    before = []
    for c in range(chunks):
        before = call(
            functools.partial(
                space_kernel, distances=early + late, late=len(late), groups=tm, first=c * step
            ),
            "spatial",
            [(rows // chunks, width) if c < chunks - 1 else (space * tm, block, width)],
            *[parts[k] for k in early],
            *ends[c],
            *qkv,
            *before,
            w_spatial,
            leave_space,
            scratch=[
                pltpu.VMEM((rows // chunks, width), BF16),
                pltpu.VMEM((3, len(late), step, toks, width), BF16),
            ],
            flops=2 * cost // chunks,
        )
    after = before[0]
    after = lax.all_to_all(after, ("space", "tm"), split_axis=0, concat_axis=0, tiled=True)
    both = [k for k in range(tm // 2) if k.bit_count() != 1]
    direct = [2 * k + s for s in range(2) for k in reversed(range(tm // 2)) if k not in both]
    result = call(
        functools.partial(time_kernel, toks=share, both=both, direct=direct),
        "temporal",
        [(2, rows // tm, width)] * len(both) + [(rows // tm, width)] * len(direct),
        after.reshape(space, tm, block, width),
        w_temporal,
        enter_time,
        scratch=[
            pltpu.VMEM((3, rows, width), BF16),
            pltpu.VMEM((rows, width), BF16),
            pltpu.VMEM((rows, width), BF16),
        ],
        flops=5 * cost,
    )

    def over_tm(part, distance):
        return lax.ppermute(part, "tm", [(i, i ^ distance) for i in range(tm)])

    whole = [over_tm(part, 2 * k) if k else part for k, part in zip(both, result)]
    pairs = [[i, i + 1] for i in range(0, tm, 2)]
    beside = [lax.all_gather(whole[0][1], "tm", axis_index_groups=pairs)]
    beside += [over_tm(part[1], 1) for part in whole[1:]]
    near = [over_tm(part, k) for k, part in zip(direct, result[len(both) :])]
    steps = 4 if frames % 4 == 0 else 1
    return call(
        functools.partial(place_kernel, both=both, direct=direct),
        "place",
        [(frames, toks, width)],
        *whole,
        *beside,
        *near,
        leave_time,
        out_specs=[pl.BlockSpec(memory_space=pl.ANY)],
        scratch=[
            pltpu.VMEM((frames, toks, width), BF16),
            pltpu.SemaphoreType.DMA((steps,)),
        ],
    )[0]


def solution(mesh):
    placed = (P("tm", "space", None), P(), P())
    return jax.shard_map(
        on_device, mesh=mesh, in_specs=placed, out_specs=P("tm", "space", None), check_vma=False
    )
```

```python
import functools
import math

import jax
import jax.numpy as jnp
from jax import lax
from jax.experimental import pallas as pl
from jax.experimental.pallas import tpu as pltpu
from jax.sharding import PartitionSpec as P

HEAD = 64
PAIR = 2 * HEAD
SCALE = math.log2(math.e) / math.sqrt(HEAD)
F32, BF16 = jnp.float32, jnp.bfloat16
MIB = 1024 * 1024


def dot(a, b):
    return jnp.dot(a, b, preferred_element_type=F32)


def rms_norm(values):
    wide = values.astype(F32)
    return (wide * lax.rsqrt(jnp.mean(wide * wide, axis=-1, keepdims=True) + 1e-06)).astype(BF16)


def halves(rows):
    first = lax.broadcasted_iota(jnp.int32, (rows, PAIR), 1) < HEAD
    one, zero = jnp.ones((rows, PAIR), F32), jnp.zeros((rows, PAIR), F32)
    return jnp.where(first, one, zero).astype(BF16), jnp.where(first, zero, one).astype(BF16)


def digits(number, *sizes):
    found = []
    for size in reversed(sizes):
        found.append(number & (size - 1))
        number = number >> (size.bit_length() - 1)
    return found[::-1]


def orders(rows, *, count, groups, share):
    toks, frames = groups * share, rows // (groups * share)
    per = frames // count

    def leave_space(row):
        k, g, f, t = digits(row, count, groups, per, share)
        return f * count * toks + k * toks + g * share + t

    def enter_time(row):
        t, m, s, i = digits(row, share, groups, count, per)
        return ((s * groups + m) * per + i) * share + t

    def leave_time(row, me):
        f, g, t = digits(row, frames, groups, share)
        return ((g ^ me) * share + t) * frames + f

    return leave_space, enter_time, leave_time


def table_kernel(_, *out_refs, **sizes):
    leave_space, enter_time, leave_time = orders(out_refs[0].shape[0], **sizes)
    me = lax.axis_index("tm")
    for out_ref, source in zip(out_refs, (leave_space, enter_time, lambda r: leave_time(r, me))):
        shape = out_ref.shape
        wanted = source(lax.broadcasted_iota(jnp.int32, (shape[0], 1), 0))
        place = lax.broadcasted_iota(jnp.int32, shape, 1)
        out_ref[...] = jnp.where(place == wanted, 1.0, 0.0).astype(BF16)


def group_of(width):
    return 2 * PAIR if width % (2 * PAIR) == 0 else PAIR


def attend(query, key, value, masks, allowed):
    rows, width = query.shape
    low, high = masks
    pairs = [slice(p, p + PAIR) for p in range(0, width, PAIR)]
    both = jnp.concatenate(
        [jnp.concatenate([query[:, p] * m for p in pairs], axis=1) for m in masks], axis=0
    )
    nothing = jnp.zeros((rows, PAIR), BF16)
    keys = jnp.concatenate(
        [
            jnp.concatenate([key[:, p] if p == q else nothing for p in pairs], axis=1)
            for q in pairs
        ],
        axis=0,
    )
    scores = lax.dot_general(both, keys, (((1,), (1,)), ((), ())), preferred_element_type=F32)
    out = []
    for i, p in enumerate(pairs):
        part = scores[:, i * rows : (i + 1) * rows]
        if allowed is not None:
            part = jnp.where(allowed, part, -1e30)
        largest = jnp.max(part, axis=-1, keepdims=True)
        expo = jnp.exp2((part - largest) * SCALE).astype(BF16)
        side = jnp.concatenate([expo[:rows], expo[rows:]], axis=1)
        right = jnp.concatenate(
            [jnp.concatenate([value[:, p] * m, m], axis=1) for m in masks], axis=0
        )
        mixed = dot(side, right)
        out.append((mixed[:, :PAIR] / mixed[:, PAIR:]).astype(BF16))
    return jnp.concatenate(out, axis=1)


def own_or_whole(clip_ref, frame):
    if len(clip_ref.shape) == 4:
        return clip_ref[lax.axis_index("space"), frame]
    return clip_ref[frame]


def project_kernel(*refs):
    *clip_refs, w_ref, out_ref = refs
    project(clip_refs, w_ref, out_ref)


def project(clip_refs, w_ref, out_ref):
    frames, toks, width = out_ref.shape[2:]
    clip = [own_or_whole(c, slice(None)).reshape(-1, width) for c in clip_refs]
    normed = rms_norm(jnp.concatenate(clip, axis=0))
    for j in range(3):
        out = dot(normed, w_ref[j]).astype(BF16)
        out_ref[j] = out.reshape(len(clip_refs), frames, toks, width)


def space_kernel(*refs, distances, late, groups, first):
    count = len(distances)
    clip_refs, refs = refs[:count], refs[count:]
    *refs, w_ref, order_ref, out_ref, mix_ref, last_ref = refs
    before = refs[len(refs) - late - 1 :] if first else []
    qkv_refs = refs[: len(refs) - len(before)]
    project(clip_refs[count - late :], w_ref, last_ref)
    frames, toks, width = last_ref.shape[2:]
    rows = count * toks
    share = toks // groups
    masks = halves(rows)
    group = group_of(width)

    def part(j, f, cols):
        early = [ref[j, s, first + f, :, cols] for ref in qkv_refs for s in range(ref.shape[1])]
        return jnp.concatenate(early + [last_ref[j, s, f, :, cols] for s in range(late)], axis=0)

    for f in range(frames):
        for p in range(0, width, group):
            cols = pl.ds(p, group)
            mixed = attend(part(0, f, cols), part(1, f, cols), part(2, f, cols), masks, None)
            mix_ref[pl.ds(f * rows, rows), cols] = mixed
    if len(out_ref.shape) == 2:
        out_ref[...] = mix_ref[...]
        return
    mix = mix_ref[...]
    if first:
        mix = jnp.concatenate([before[0][...], mix], axis=0)

    def block_of(i, f):
        if i < count - late:
            return own_or_whole(clip_refs[i], f)
        if f < first:
            return before[1 + i - count + late][f]
        return clip_refs[i][f - first]

    clip = [block_of(i, f) for f in range(first + frames) for i in range(count)]
    after = dot(mix, w_ref[3]) + jnp.concatenate(clip, axis=0).astype(F32)
    after = after.astype(BF16)
    after = dot(order_ref[...], after).astype(BF16).reshape(count, groups, -1, width)
    me = lax.axis_index("space")
    for i, k in enumerate(distances):
        out_ref[pl.ds((me ^ k) * groups, groups)] = after[i]


def time_kernel(x_ref, w_ref, order_ref, *refs, toks, both, direct):
    *out_refs, qkv_ref, mix_ref, done_ref = refs
    space, groups, block, width = x_ref.shape
    rows = space * groups * block
    frames = rows // toks
    masks = halves(frames)
    group = group_of(width)

    x = dot(order_ref[...], x_ref[...].reshape(rows, width)).astype(BF16)
    normed = rms_norm(x)
    for j in range(3):
        qkv_ref[j] = dot(normed, w_ref[j]).astype(BF16)
    order = lax.broadcasted_iota(jnp.int32, (2 * frames, frames), 0) & (frames - 1)
    allowed = lax.broadcasted_iota(jnp.int32, (2 * frames, frames), 1) <= order
    for t in range(toks):
        at = pl.ds(t * frames, frames)
        for p in range(0, width, group):
            cols = pl.ds(p, group)
            mix_ref[at, cols] = attend(
                qkv_ref[0, at, cols], qkv_ref[1, at, cols], qkv_ref[2, at, cols], masks, allowed
            )
    done_ref[...] = (dot(mix_ref[...], w_ref[3]) + x.astype(F32)).astype(BF16)
    me = lax.axis_index("tm")
    own = frames // groups
    for k in range(groups):
        for t in range(toks):
            at = pl.multiple_of(t * frames + (me ^ k) * own, own)
            block = done_ref[pl.ds(at, own), :]
            if k // 2 in both:
                out_refs[both.index(k // 2)][k % 2, pl.ds(t * own, own), :] = block
            else:
                out_refs[len(both) + direct.index(k)][pl.ds(t * own, own), :] = block


def place_kernel(*refs, both, direct):
    *in_refs, order_ref, out_ref, done_ref, sems = refs
    frames, toks, width = out_ref.shape
    parts = {2 * k: in_refs[i].at[0] for i, k in enumerate(both)}
    parts |= {2 * k + 1: in_refs[len(both) + i] for i, k in enumerate(both)}
    parts[1] = parts[1].at[1 - lax.axis_index("tm") % 2]
    parts |= {k: in_refs[2 * len(both) + i] for i, k in enumerate(direct)}
    rows = jnp.concatenate([parts[k][...] for k in range(len(parts))], axis=0)
    steps = sems.shape[0]
    some = frames // steps
    copies = []
    for step in range(steps):
        at = pl.ds(step * some, some)
        done = dot(order_ref[pl.ds(step * some * toks, some * toks), :], rows).astype(BF16)
        done_ref[at] = done.reshape(some, toks, width)
        copies.append(pltpu.make_async_copy(done_ref.at[at], out_ref.at[at], sems.at[step]))
        copies[-1].start()
    for copy in copies:
        copy.wait()


def call(kernel, name, outs, *args, scratch=(), flops=0, **blocks):
    like = [jax.ShapeDtypeStruct(shape, BF16) for shape in outs]
    size = 2 * sum(math.prod(a.shape) for a in (*args, *like))
    within = pl.BlockSpec(memory_space=pltpu.VMEM)
    return pl.pallas_call(
        kernel,
        out_shape=like,
        in_specs=[within] * len(args),
        out_specs=blocks.pop("out_specs", [within] * len(outs)),
        scratch_shapes=scratch,
        compiler_params=pltpu.CompilerParams(vmem_limit_bytes=20 * MIB),
        cost_estimate=pl.CostEstimate(flops=flops, bytes_accessed=size, transcendentals=0),
        name=name,
        **blocks,
    )(*args)


def on_device(clip, w_spatial, w_temporal):
    frames, toks, width = clip.shape
    rows = frames * toks
    tm, space = lax.axis_size("tm"), lax.axis_size("space")
    share = toks // tm
    per = frames // space
    block = per * share
    piece = (per, toks, width)
    cost = 2 * rows * width * width

    blocks = clip.reshape(space, *piece)
    me = lax.axis_index("space")
    early = [0, 2, 1] if space > 3 else [0]
    late = [k for k in range(space) if k not in early]
    chunks = 2 if per % 2 == 0 and late else 1
    step = per // chunks
    parts = {0: blocks}
    held = blocks
    for k in early[1:] + late:
        parts[k] = lax.dynamic_index_in_dim(held, me ^ k, 0, keepdims=False)
        held = lax.optimization_barrier((blocks, parts[k]))[0]

    def over_space(part, distance):
        return lax.ppermute(part, "space", [(i, i ^ distance) for i in range(space)])

    for k in early[1:]:
        parts[k] = over_space(parts[k], k)
    ends = [
        [over_space(parts[k][c * step : (c + 1) * step], k) for k in late] for c in range(chunks)
    ]
    groups = [[k] for k in early]
    qkv = [
        call(
            project_kernel,
            "project",
            [(3, len(group), *piece)],
            *[parts[k] for k in group],
            w_spatial,
            flops=3 * cost * len(group) // space,
        )[0]
        for group in groups
    ]
    leave_space, enter_time, leave_time = call(
        functools.partial(
            table_kernel, count=space, groups=tm, share=share
        ),
        "orders",
        [(rows, rows)] * 3,
        qkv[0],
    )
    before = []
    for c in range(chunks):
        before = call(
            functools.partial(
                space_kernel, distances=early + late, late=len(late), groups=tm, first=c * step
            ),
            "spatial",
            [(rows // chunks, width) if c < chunks - 1 else (space * tm, block, width)],
            *[parts[k] for k in early],
            *ends[c],
            *qkv,
            *before,
            *(ends[0] if c else []),
            w_spatial,
            leave_space,
            scratch=[
                pltpu.VMEM((rows // chunks, width), BF16),
                pltpu.VMEM((3, len(late), step, toks, width), BF16),
            ],
            flops=2 * cost // chunks,
        )
    after = before[0]
    after = lax.all_to_all(after, ("space", "tm"), split_axis=0, concat_axis=0, tiled=True)
    both = [k for k in range(tm // 2) if k.bit_count() != 1]
    direct = [2 * k + s for s in range(2) for k in reversed(range(tm // 2)) if k not in both]
    result = call(
        functools.partial(time_kernel, toks=share, both=both, direct=direct),
        "temporal",
        [(2, rows // tm, width)] * len(both) + [(rows // tm, width)] * len(direct),
        after.reshape(space, tm, block, width),
        w_temporal,
        enter_time,
        scratch=[
            pltpu.VMEM((3, rows, width), BF16),
            pltpu.VMEM((rows, width), BF16),
            pltpu.VMEM((rows, width), BF16),
        ],
        flops=5 * cost,
    )

    def over_tm(part, distance):
        return lax.ppermute(part, "tm", [(i, i ^ distance) for i in range(tm)])

    whole = [over_tm(part, 2 * k) if k else part for k, part in zip(both, result)]
    pairs = [[i, i + 1] for i in range(0, tm, 2)]
    beside = [lax.all_gather(whole[0][1], "tm", axis_index_groups=pairs)]
    beside += [over_tm(part[1], 1) for part in whole[1:]]
    near = [over_tm(part, k) for k, part in zip(direct, result[len(both) :])]
    steps = 4 if frames % 4 == 0 else 1
    return call(
        functools.partial(place_kernel, both=both, direct=direct),
        "place",
        [(frames, toks, width)],
        *whole,
        *beside,
        *near,
        leave_time,
        out_specs=[pl.BlockSpec(memory_space=pl.ANY)],
        scratch=[
            pltpu.VMEM((frames, toks, width), BF16),
            pltpu.SemaphoreType.DMA((steps,)),
        ],
    )[0]


def solution(mesh):
    placed = (P("tm", "space", None), P(), P())
    return jax.shard_map(
        on_device, mesh=mesh, in_specs=placed, out_specs=P("tm", "space", None), check_vma=False
    )
```

```python
import functools
import math

import jax
import jax.numpy as jnp
from jax import lax
from jax.experimental import pallas as pl
from jax.experimental.pallas import tpu as pltpu
from jax.sharding import PartitionSpec as P

HEAD = 64
PAIR = 2 * HEAD
SCALE = math.log2(math.e) / math.sqrt(HEAD)
F32, BF16 = jnp.float32, jnp.bfloat16
MIB = 1024 * 1024


def dot(a, b):
    return jnp.dot(a, b, preferred_element_type=F32)


def rms_norm(values):
    wide = values.astype(F32)
    return (wide * lax.rsqrt(jnp.mean(wide * wide, axis=-1, keepdims=True) + 1e-06)).astype(BF16)


def halves(rows):
    first = lax.broadcasted_iota(jnp.int32, (rows, PAIR), 1) < HEAD
    one, zero = jnp.ones((rows, PAIR), F32), jnp.zeros((rows, PAIR), F32)
    return jnp.where(first, one, zero).astype(BF16), jnp.where(first, zero, one).astype(BF16)


def digits(number, *sizes):
    found = []
    for size in reversed(sizes):
        found.append(number & (size - 1))
        number = number >> (size.bit_length() - 1)
    return found[::-1]


def orders(rows, *, count, groups, share):
    toks, frames = groups * share, rows // (groups * share)
    per = frames // count

    def leave_space(row):
        k, g, f, t = digits(row, count, groups, per, share)
        return f * count * toks + k * toks + g * share + t

    def enter_time(row):
        t, m, s, i = digits(row, share, groups, count, per)
        return ((s * groups + m) * per + i) * share + t

    def leave_time(row, me):
        f, g, t = digits(row, frames, groups, share)
        return ((g ^ me) * share + t) * frames + f

    return leave_space, enter_time, leave_time


def table_kernel(_, *out_refs, **sizes):
    leave_space, enter_time, leave_time = orders(out_refs[0].shape[0], **sizes)
    me = lax.axis_index("tm")
    for out_ref, source in zip(out_refs, (leave_space, enter_time, lambda r: leave_time(r, me))):
        shape = out_ref.shape
        wanted = source(lax.broadcasted_iota(jnp.int32, (shape[0], 1), 0))
        place = lax.broadcasted_iota(jnp.int32, shape, 1)
        out_ref[...] = jnp.where(place == wanted, 1.0, 0.0).astype(BF16)


def group_of(width):
    return 2 * PAIR if width % (2 * PAIR) == 0 else PAIR


def attend(query, key, value, masks, allowed):
    rows, width = query.shape
    low, high = masks
    pairs = [slice(p, p + PAIR) for p in range(0, width, PAIR)]
    both = jnp.concatenate(
        [jnp.concatenate([query[:, p] * m for p in pairs], axis=1) for m in masks], axis=0
    )
    nothing = jnp.zeros((rows, PAIR), BF16)
    keys = jnp.concatenate(
        [
            jnp.concatenate([key[:, p] if p == q else nothing for p in pairs], axis=1)
            for q in pairs
        ],
        axis=0,
    )
    scores = lax.dot_general(both, keys, (((1,), (1,)), ((), ())), preferred_element_type=F32)
    out = []
    for i, p in enumerate(pairs):
        part = scores[:, i * rows : (i + 1) * rows]
        if allowed is not None:
            part = jnp.where(allowed, part, -1e30)
        largest = jnp.max(part, axis=-1, keepdims=True)
        expo = jnp.exp2((part - largest) * SCALE).astype(BF16)
        side = jnp.concatenate([expo[:rows], expo[rows:]], axis=1)
        right = jnp.concatenate(
            [jnp.concatenate([value[:, p] * m, m], axis=1) for m in masks], axis=0
        )
        mixed = dot(side, right)
        out.append((mixed[:, :PAIR] / mixed[:, PAIR:]).astype(BF16))
    return jnp.concatenate(out, axis=1)


def own_or_whole(clip_ref, frame):
    if len(clip_ref.shape) == 4:
        return clip_ref[lax.axis_index("space"), frame]
    return clip_ref[frame]


def project_kernel(*refs):
    *clip_refs, w_ref, out_ref = refs
    project(clip_refs, w_ref, out_ref)


def project(clip_refs, w_ref, out_ref):
    frames, toks, width = out_ref.shape[2:]
    clip = [own_or_whole(c, slice(None)).reshape(-1, width) for c in clip_refs]
    normed = rms_norm(jnp.concatenate(clip, axis=0))
    for j in range(3):
        out = dot(normed, w_ref[j]).astype(BF16)
        out_ref[j] = out.reshape(len(clip_refs), frames, toks, width)


def space_kernel(*refs, distances, late, groups, first):
    count = len(distances)
    clip_refs, refs = refs[:count], refs[count:]
    *refs, w_ref, order_ref, out_ref, mix_ref, last_ref = refs
    qkv_refs, before = (refs[:-1], refs[-1]) if first else (refs, None)
    project(clip_refs[count - late :], w_ref, last_ref)
    frames, toks, width = last_ref.shape[2:]
    rows = count * toks
    share = toks // groups
    masks = halves(rows)
    group = group_of(width)

    def part(j, f, cols):
        early = [ref[j, s, first + f, :, cols] for ref in qkv_refs for s in range(ref.shape[1])]
        return jnp.concatenate(early + [last_ref[j, s, f, :, cols] for s in range(late)], axis=0)

    for f in range(frames):
        for p in range(0, width, group):
            cols = pl.ds(p, group)
            mixed = attend(part(0, f, cols), part(1, f, cols), part(2, f, cols), masks, None)
            mix_ref[pl.ds(f * rows, rows), cols] = mixed
    clip = [
        own_or_whole(c, f if i >= count - late else first + f)
        for f in range(frames)
        for i, c in enumerate(clip_refs)
    ]
    after = dot(mix_ref[...], w_ref[3]) + jnp.concatenate(clip, axis=0).astype(F32)
    after = after.astype(BF16)
    if len(out_ref.shape) == 2:
        out_ref[...] = after
        return
    if before is not None:
        after = jnp.concatenate([before[...], after], axis=0)
    after = dot(order_ref[...], after).astype(BF16).reshape(count, groups, -1, width)
    me = lax.axis_index("space")
    for i, k in enumerate(distances):
        out_ref[pl.ds((me ^ k) * groups, groups)] = after[i]


def time_kernel(x_ref, w_ref, order_ref, *refs, toks, both, direct):
    *out_refs, qkv_ref, mix_ref, done_ref = refs
    space, groups, block, width = x_ref.shape
    rows = space * groups * block
    frames = rows // toks
    masks = halves(frames)
    group = group_of(width)

    x = dot(order_ref[...], x_ref[...].reshape(rows, width)).astype(BF16)
    normed = rms_norm(x)
    for j in range(3):
        qkv_ref[j] = dot(normed, w_ref[j]).astype(BF16)
    order = lax.broadcasted_iota(jnp.int32, (2 * frames, frames), 0) & (frames - 1)
    allowed = lax.broadcasted_iota(jnp.int32, (2 * frames, frames), 1) <= order
    for t in range(toks):
        at = pl.ds(t * frames, frames)
        for p in range(0, width, group):
            cols = pl.ds(p, group)
            mix_ref[at, cols] = attend(
                qkv_ref[0, at, cols], qkv_ref[1, at, cols], qkv_ref[2, at, cols], masks, allowed
            )
    done_ref[...] = (dot(mix_ref[...], w_ref[3]) + x.astype(F32)).astype(BF16)
    me = lax.axis_index("tm")
    own = frames // groups
    for k in range(groups):
        for t in range(toks):
            at = pl.multiple_of(t * frames + (me ^ k) * own, own)
            block = done_ref[pl.ds(at, own), :]
            if k // 2 in both:
                out_refs[both.index(k // 2)][k % 2, pl.ds(t * own, own), :] = block
            else:
                out_refs[len(both) + direct.index(k)][pl.ds(t * own, own), :] = block


def place_kernel(*refs, both, direct):
    *in_refs, order_ref, out_ref, done_ref, sems = refs
    frames, toks, width = out_ref.shape
    parts = {2 * k: in_refs[i].at[0] for i, k in enumerate(both)}
    other = in_refs[len(both)].at[1 - lax.axis_index("tm") % 2]
    parts |= {2 * k + 1: other.at[i] for i, k in enumerate(both)}
    parts |= {k: in_refs[len(both) + 1 + i] for i, k in enumerate(direct)}
    rows = jnp.concatenate([parts[k][...] for k in range(len(parts))], axis=0)
    steps = sems.shape[0]
    some = frames // steps
    copies = []
    for step in range(steps):
        at = pl.ds(step * some, some)
        done = dot(order_ref[pl.ds(step * some * toks, some * toks), :], rows).astype(BF16)
        done_ref[at] = done.reshape(some, toks, width)
        copies.append(pltpu.make_async_copy(done_ref.at[at], out_ref.at[at], sems.at[step]))
        copies[-1].start()
    for copy in copies:
        copy.wait()


def call(kernel, name, outs, *args, scratch=(), flops=0, **blocks):
    like = [jax.ShapeDtypeStruct(shape, BF16) for shape in outs]
    size = 2 * sum(math.prod(a.shape) for a in (*args, *like))
    within = pl.BlockSpec(memory_space=pltpu.VMEM)
    return pl.pallas_call(
        kernel,
        out_shape=like,
        in_specs=[within] * len(args),
        out_specs=blocks.pop("out_specs", [within] * len(outs)),
        scratch_shapes=scratch,
        compiler_params=pltpu.CompilerParams(vmem_limit_bytes=20 * MIB),
        cost_estimate=pl.CostEstimate(flops=flops, bytes_accessed=size, transcendentals=0),
        name=name,
        **blocks,
    )(*args)


def on_device(clip, w_spatial, w_temporal):
    frames, toks, width = clip.shape
    rows = frames * toks
    tm, space = lax.axis_size("tm"), lax.axis_size("space")
    share = toks // tm
    per = frames // space
    block = per * share
    piece = (per, toks, width)
    cost = 2 * rows * width * width

    blocks = clip.reshape(space, *piece)
    me = lax.axis_index("space")
    early = [0, 2, 1] if space > 3 else [0]
    late = [k for k in range(space) if k not in early]
    chunks = 2 if per % 2 == 0 and late else 1
    step = per // chunks
    parts = {0: blocks}
    held = blocks
    for k in early[1:] + late:
        parts[k] = lax.dynamic_index_in_dim(held, me ^ k, 0, keepdims=False)
        held = lax.optimization_barrier((blocks, parts[k]))[0]

    def over_space(part, distance):
        return lax.ppermute(part, "space", [(i, i ^ distance) for i in range(space)])

    for k in early[1:]:
        parts[k] = over_space(parts[k], k)
    ends = [
        [over_space(parts[k][c * step : (c + 1) * step], k) for k in late] for c in range(chunks)
    ]
    groups = [[k] for k in early]
    qkv = [
        call(
            project_kernel,
            "project",
            [(3, len(group), *piece)],
            *[parts[k] for k in group],
            w_spatial,
            flops=3 * cost * len(group) // space,
        )[0]
        for group in groups
    ]
    leave_space, enter_time, leave_time = call(
        functools.partial(
            table_kernel, count=space, groups=tm, share=share
        ),
        "orders",
        [(rows, rows)] * 3,
        qkv[0],
    )
    before = []
    for c in range(chunks):
        before = call(
            functools.partial(
                space_kernel, distances=early + late, late=len(late), groups=tm, first=c * step
            ),
            "spatial",
            [(rows // chunks, width) if c < chunks - 1 else (space * tm, block, width)],
            *[parts[k] for k in early],
            *ends[c],
            *qkv,
            *before,
            w_spatial,
            leave_space,
            scratch=[
                pltpu.VMEM((rows // chunks, width), BF16),
                pltpu.VMEM((3, len(late), step, toks, width), BF16),
            ],
            flops=2 * cost // chunks,
        )
    after = before[0]
    after = lax.all_to_all(after, ("space", "tm"), split_axis=0, concat_axis=0, tiled=True)
    both = [k for k in range(tm // 2) if k.bit_count() != 1]
    direct = [2 * k + s for s in range(2) for k in reversed(range(tm // 2)) if k not in both]
    result = call(
        functools.partial(time_kernel, toks=share, both=both, direct=direct),
        "temporal",
        [(2, rows // tm, width)] * len(both) + [(rows // tm, width)] * len(direct),
        after.reshape(space, tm, block, width),
        w_temporal,
        enter_time,
        scratch=[
            pltpu.VMEM((3, rows, width), BF16),
            pltpu.VMEM((rows, width), BF16),
            pltpu.VMEM((rows, width), BF16),
        ],
        flops=5 * cost,
    )

    def over_tm(part, distance):
        return lax.ppermute(part, "tm", [(i, i ^ distance) for i in range(tm)])

    whole = [over_tm(part, 2 * k) if k else part for k, part in zip(both, result)]
    pairs = [[i, i + 1] for i in range(0, tm, 2)]
    beside = jnp.stack([part[1] for part in whole])
    beside = [lax.all_gather(beside, "tm", axis_index_groups=pairs)]
    near = [over_tm(part, k) for k, part in zip(direct, result[len(both) :])]
    steps = 2 if frames % 2 == 0 else 1
    return call(
        functools.partial(place_kernel, both=both, direct=direct),
        "place",
        [(frames, toks, width)],
        *whole,
        *beside,
        *near,
        leave_time,
        out_specs=[pl.BlockSpec(memory_space=pl.ANY)],
        scratch=[
            pltpu.VMEM((frames, toks, width), BF16),
            pltpu.SemaphoreType.DMA((steps,)),
        ],
    )[0]


def solution(mesh):
    placed = (P("tm", "space", None), P(), P())
    return jax.shard_map(
        on_device, mesh=mesh, in_specs=placed, out_specs=P("tm", "space", None), check_vma=False
    )
```
